32 devices in a mesh: tm: 8 (over z, y), member: 4 (over x, core).
Axes of the slice: x: 2, y: 2, z: 4, core: 2. Of those that a mesh axis runs over, the one named last changes fastest.
Arguments:
- queries: bfloat16 [16384, 512], P(('member', 'tm')), parts along dimension 0, may hold values from -12 to 12
- key_rows: bfloat16 [16384, 512], P(('member', 'tm')), parts along dimension 0, may hold values from -6 to 6
- value_rows: bfloat16 [16384, 512], P(('member', 'tm')), parts along dimension 0, may hold values from -6 to 6
- grad_output: bfloat16 [16384, 512], P(('member', 'tm')), parts along dimension 0, may hold values from -6 to 6
- extra_blocks: int32 [32, 16], P('member'), parts along dimension 0, may hold values from -1 to 255, as said below
Outputs:
- mixed_rows: bfloat16 [16384, 512], P(('member', 'tm')), parts along dimension 0
- query_grad: bfloat16 [16384, 512], P(('member', 'tm')), parts along dimension 0
- key_grad: bfloat16 [16384, 512], P(('member', 'tm')), parts along dimension 0
- value_grad: bfloat16 [16384, 512], P(('member', 'tm')), parts along dimension 0
The draws below stay inside these ranges and needn't reach their ends.
There are 4 independent parts, one for each index of `member`. The reference program is written for one: setup_inputs(seed, part) draws one part's arguments, and reference() takes and returns one part's arrays. A program takes and returns all parts, laid end to end along the dimension named above; each array names one. Nothing has to cross between parts.
Inputs may be any that keep to these rules, and one draw needn't show every extreme that they name: `extra_blocks`: row b lists distinct sub-blocks of 16 rows, each inside an earlier block; -1 marks an empty entry, and empty entries stand after the others. From any one block a row takes either no sub-block or exactly 2.
All inputs are finite; a program needn't handle non-finite values.
Results may differ from the reference program's by a relative error of at most 0.035.
Values may be sent and summed in bfloat16 or wider, within the bound.
No kernel may reach another device: no remote copies, remote signals or barrier semaphores. Data moves between devices by JAX's collectives and lax.ppermute only.
A program may use at most 128 MiB of HBM per device.

```python
import math
import jax
import jax.numpy as jnp
from jax import lax

H = 8
HD = 64
HG = 2
BLK = 512
SUB = 16
EXTRA = 16
CAP = 2
D = 512
SEQ = 4096
N_TM = 8


def draw_queries(key, part):
    return jnp.clip(2.0 * jax.random.normal(jax.random.fold_in(key, 1), (SEQ, H * HD), jnp.float32), -12.0, 12.0).astype(jnp.bfloat16)


def draw_key_rows(key, part):
    return jnp.clip(jax.random.normal(jax.random.fold_in(key, 2), (SEQ, H * HD), jnp.float32), -6.0, 6.0).astype(jnp.bfloat16)


def draw_extra_blocks(key, part):
    block_count = N_TM
    per_block = BLK // SUB
    owners_each = EXTRA // CAP
    block_ids = jnp.arange(block_count, dtype=jnp.int32)
    block_gap = block_ids[:, None] - block_ids[None, :]
    usable = block_gap > 0
    last_row = block_ids[:, None] == block_count - 1
    second_row = block_ids[:, None] == block_count - 2
    forced = last_row & ((block_ids[None, :] == block_count - 2) | (block_ids[None, :] == 0)) | second_row & (block_ids[None, :] == block_count // 2 - 2)
    hot_key, score_key, inside_key = jax.random.split(jax.random.fold_in(key, 3), 3)
    popular = jax.random.randint(hot_key, (block_count,), 0, 4) == 0
    raw_scores = jax.random.randint(score_key, (block_count, block_count), 0, 1000) + 1500 * popular.astype(jnp.int32)[None, :] + 100000 * forced.astype(jnp.int32)
    ranked = jnp.where(usable, raw_scores * block_count + block_ids[None, :], -1 - block_ids[None, :])
    top_scores, owners = lax.top_k(ranked, owners_each)
    picked = top_scores >= 0
    inside_scores = jax.random.randint(inside_key, (block_count, owners_each, per_block), 0, 65536) * per_block + jnp.arange(per_block, dtype=jnp.int32)
    inside_top, inside = lax.top_k(inside_scores, CAP)
    entries = owners[:, :, None] * per_block + inside
    entries = jnp.where(picked[:, :, None], entries, -1)
    return entries.reshape(block_count, EXTRA).astype(jnp.int32)


def levels(stream_key, shape, shards, low, top_value):
    level, own = 1.0, jax.random.fold_in(stream_key, 6)
    for position, blocks in shards:
        draws = jnp.exp(jax.random.uniform(jax.random.fold_in(own, position), (blocks,), jnp.float32, low / len(shards), top_value / len(shards)))
        level = level * jnp.repeat(draws, shape[position] // blocks).reshape([-1 if axis == position else 1 for axis in range(len(shape))])
    return level


def centred(key, dims, spread, bound, cuts=(), kind=jnp.bfloat16):
    loudness = levels(key, dims, cuts, -0.22, 0.18) if cuts else 1.0
    result = jax.random.normal(key, dims, jnp.float32) * spread * loudness
    return jnp.minimum(jnp.maximum(result, -bound), bound).astype(kind)


def setup_inputs(seed: int = 0, part: int = 0) -> dict:
    splits = jax.random.split(jax.random.key(seed), 6)
    part_keys = jax.random.split(jax.random.fold_in(splits[5], part), 6)
    return {
        "queries": draw_queries(jax.random.fold_in(jax.random.fold_in(splits[5], part), 71), part),
        "key_rows": draw_key_rows(jax.random.fold_in(jax.random.fold_in(splits[5], part), 71), part),
        "value_rows": centred(part_keys[2], (SEQ, D), 1.0, 6.0, ((0, 8),)),
        "grad_output": centred(part_keys[3], (SEQ, D), 1.0, 6.0, ((0, 8),)),
        "extra_blocks": draw_extra_blocks(jax.random.fold_in(jax.random.fold_in(splits[5], part), 71), part),
    }


very_negative = -1e+30

def rounded(values):
    return lax.optimization_barrier(values.astype(jnp.bfloat16)).astype(jnp.float32)

def split_heads(values):
    return values.reshape(values.shape[0], values.shape[1] // HD, HD).astype(jnp.float32)

def forward_group(query_part, key_part, value_part, key_mask, scaling):
    scores = jnp.einsum('qhd,khd->hqk', split_heads(query_part), split_heads(key_part)) * scaling
    scores = jnp.where(key_mask[None], scores, very_negative)
    weights = jax.nn.softmax(scores, axis=-1)
    weights_low = weights.astype(jnp.bfloat16)
    mixed_heads = jnp.einsum('hqk,khd->qhd', weights_low.astype(jnp.float32), split_heads(value_part))
    mixed_part = mixed_heads.reshape(query_part.shape).astype(jnp.bfloat16)
    return (weights, weights_low, mixed_part)

def backward_group(query_part, key_part, value_part, grad_part, mixed_part, weights, weights_low, scaling):
    grad_heads = split_heads(grad_part)
    row_delta = lax.optimization_barrier(jnp.sum(grad_heads * split_heads(mixed_part), axis=-1))
    row_delta = jnp.transpose(row_delta)[:, :, None]
    weight_grads = jnp.einsum('qhd,khd->hqk', grad_heads, split_heads(value_part))
    score_grads = (weights * (weight_grads - row_delta)).astype(jnp.bfloat16).astype(jnp.float32)
    query_grads = jnp.einsum('hqk,khd->qhd', score_grads, split_heads(key_part)) * scaling
    key_grads = jnp.einsum('hqk,qhd->khd', score_grads, split_heads(query_part)) * scaling
    value_grads = jnp.einsum('hqk,qhd->khd', weights_low.astype(jnp.float32), grad_heads)
    return (query_grads.reshape(query_part.shape), key_grads.reshape(key_part.shape), value_grads.reshape(key_part.shape))

def reference(queries, key_rows, value_rows, grad_output, extra_blocks):
    model_width = queries.shape[1]
    group_width = HG * HD
    group_count = model_width // group_width
    scaling = 1.0 / math.sqrt(HD)
    distances = []
    reach = 1
    while reach < N_TM:
        distances.append(reach)
        reach = reach * 2
    row_ids = jnp.arange(BLK, dtype=jnp.int32)
    own_mask = row_ids[:, None] >= row_ids[None, :]
    key_table = key_rows.reshape(SEQ // SUB, SUB * model_width)
    value_table = value_rows.reshape(SEQ // SUB, SUB * model_width)

    def one_block(accumulated, block_index):
        key_acc, value_acc = accumulated
        row_start = (block_index * BLK).astype(jnp.int32)
        query_block = lax.dynamic_slice_in_dim(queries, row_start, BLK, 0)
        grad_block = lax.dynamic_slice_in_dim(grad_output, row_start, BLK, 0)
        key_list = [lax.dynamic_slice_in_dim(key_rows, row_start, BLK, 0)]
        value_list = [lax.dynamic_slice_in_dim(value_rows, row_start, BLK, 0)]
        live_list = []
        other_starts = []
        for distance in distances:
            other_start = (jnp.maximum(block_index - distance, 0) * BLK).astype(jnp.int32)
            other_starts.append(other_start)
            key_list.append(lax.dynamic_slice_in_dim(key_rows, other_start, BLK, 0))
            value_list.append(lax.dynamic_slice_in_dim(value_rows, other_start, BLK, 0))
            live_list.append(jnp.broadcast_to(block_index >= distance, (BLK,)))
        entries = lax.dynamic_index_in_dim(extra_blocks, block_index, 0, keepdims=False)
        entry_live = entries >= 0
        entry_index = jnp.where(entry_live, entries, 0).astype(jnp.int32)
        key_list.append(jnp.take(key_table, entry_index, axis=0).reshape(EXTRA * SUB, model_width))
        value_list.append(jnp.take(value_table, entry_index, axis=0).reshape(EXTRA * SUB, model_width))
        live_list.append(jnp.repeat(entry_live, SUB))
        far_live = jnp.concatenate(live_list)
        key_mask = jnp.concatenate([own_mask, jnp.broadcast_to(far_live[None, :], (BLK, far_live.shape[0]))], axis=1)
        all_keys = jnp.concatenate(key_list, axis=0)
        all_values = jnp.concatenate(value_list, axis=0)
        mixed_parts, query_parts, key_parts, value_parts = ([], [], [], [])
        for group_index in range(group_count):
            low = group_index * group_width
            high = low + group_width
            weights, weights_low, mixed_part = forward_group(query_block[:, low:high], all_keys[:, low:high], all_values[:, low:high], key_mask, scaling)
            grads = backward_group(query_block[:, low:high], all_keys[:, low:high], all_values[:, low:high], grad_block[:, low:high], mixed_part, weights, weights_low, scaling)
            mixed_parts.append(mixed_part)
            query_parts.append(grads[0])
            key_parts.append(grads[1])
            value_parts.append(grads[2])
        mixed_block = jnp.concatenate(mixed_parts, axis=1)
        query_block_grad = jnp.concatenate(query_parts, axis=1).astype(jnp.bfloat16)
        key_grads = jnp.concatenate(key_parts, axis=1)
        value_grads = jnp.concatenate(value_parts, axis=1)
        key_acc = lax.dynamic_update_slice_in_dim(key_acc, lax.dynamic_slice_in_dim(key_acc, row_start, BLK, 0) + key_grads[:BLK], row_start, 0)
        value_acc = lax.dynamic_update_slice_in_dim(value_acc, lax.dynamic_slice_in_dim(value_acc, row_start, BLK, 0) + value_grads[:BLK], row_start, 0)
        for level, other_start in enumerate(other_starts):
            low = (1 + level) * BLK
            key_term = rounded(key_grads[low:low + BLK])
            value_term = rounded(value_grads[low:low + BLK])
            key_acc = lax.dynamic_update_slice_in_dim(key_acc, lax.dynamic_slice_in_dim(key_acc, other_start, BLK, 0) + key_term, other_start, 0)
            value_acc = lax.dynamic_update_slice_in_dim(value_acc, lax.dynamic_slice_in_dim(value_acc, other_start, BLK, 0) + value_term, other_start, 0)
        extra_start = (1 + len(distances)) * BLK
        key_term = rounded(key_grads[extra_start:]).reshape(EXTRA, SUB * model_width)
        value_term = rounded(value_grads[extra_start:]).reshape(EXTRA, SUB * model_width)
        key_acc = key_acc.reshape(SEQ // SUB, SUB * model_width).at[entry_index].add(key_term).reshape(SEQ, model_width)
        value_acc = value_acc.reshape(SEQ // SUB, SUB * model_width).at[entry_index].add(value_term).reshape(SEQ, model_width)
        return ((key_acc, value_acc), (mixed_block, query_block_grad))
    start_acc = (jnp.zeros((SEQ, model_width), jnp.float32), jnp.zeros((SEQ, model_width), jnp.float32))
    final_acc, outputs = lax.scan(one_block, start_acc, jnp.arange(N_TM, dtype=jnp.int32))
    mixed_rows = outputs[0].reshape(SEQ, model_width)
    query_grad = outputs[1].reshape(SEQ, model_width)
    return (mixed_rows, query_grad, final_acc[0].astype(jnp.bfloat16), final_acc[1].astype(jnp.bfloat16))
```

```python
import functools
import math

import jax
import jax.numpy as jnp
from jax import lax
from jax.experimental import pallas as pl
from jax.experimental.pallas import tpu as pltpu
from jax.sharding import PartitionSpec as P

HD = 64
HG = 2
SUB = 16
CAP = 2
TILE = 256
LOWEST = -1e30
CAST = jnp.bfloat16


very_negative = -1e30


def from_behind(value, axis, by):
    peers = lax.axis_size(axis)
    pairs = [(i, i + by) for i in range(peers) if 0 <= i + by < peers]
    return lax.ppermute(value, axis, pairs)


def split_heads(values):
    return values.reshape(values.shape[0], values.shape[1] // HD, HD)


def forward_group(query_part, key_part, value_part, key_mask, scaling):
    scores = (
        jnp.einsum(
            "qhd,khd->hqk",
            split_heads(query_part),
            split_heads(key_part),
            preferred_element_type=jnp.float32,
        )
        * scaling
    )
    scores = jnp.where(key_mask[None], scores, very_negative)
    weights = jax.nn.softmax(scores, axis=-1)
    weights_low = weights.astype(jnp.bfloat16)
    mixed_heads = jnp.einsum(
        "hqk,khd->qhd", weights_low, split_heads(value_part), preferred_element_type=jnp.float32
    )
    mixed_part = mixed_heads.reshape(query_part.shape).astype(jnp.bfloat16)
    return (weights, weights_low, mixed_part)


def backward_group(
    query_part, key_part, value_part, grad_part, mixed_part, weights, weights_low, scaling
):
    grad_heads = split_heads(grad_part)
    row_delta = jnp.sum(
        grad_heads.astype(jnp.float32) * split_heads(mixed_part).astype(jnp.float32), axis=-1
    )
    row_delta = jnp.transpose(row_delta)[:, :, None]
    weight_grads = jnp.einsum(
        "qhd,khd->hqk", grad_heads, split_heads(value_part), preferred_element_type=jnp.float32
    )
    score_grads = (weights * (weight_grads - row_delta)).astype(jnp.bfloat16)
    query_grads = (
        jnp.einsum(
            "hqk,khd->qhd", score_grads, split_heads(key_part), preferred_element_type=jnp.float32
        )
        * scaling
    )
    key_grads = (
        jnp.einsum(
            "hqk,qhd->khd", score_grads, split_heads(query_part), preferred_element_type=jnp.float32
        )
        * scaling
    )
    value_grads = jnp.einsum(
        "hqk,qhd->khd", weights_low, grad_heads, preferred_element_type=jnp.float32
    )
    return (
        query_grads.reshape(query_part.shape),
        key_grads.reshape(key_part.shape),
        value_grads.reshape(key_part.shape),
    )


def block_plan(queries, key_rows, value_rows, grad_output, extra_blocks):
    devices = lax.axis_size("tm")
    position = lax.axis_index("tm")
    block_rows = queries.shape[0]
    model_width = queries.shape[1]
    per_block = block_rows // SUB
    group_width = HG * HD
    group_count = model_width // group_width
    scaling = 1.0 / math.sqrt(HD)
    distances = []
    reach = 1
    while reach < devices:
        distances.append(reach)
        reach = reach * 2
    key_value = jnp.concatenate([key_rows, value_rows], axis=1)
    partner_blocks = [from_behind(key_value, "tm", distance) for distance in distances]
    owner_table = jnp.where(extra_blocks >= 0, extra_blocks // per_block, -1)
    inside_table = jnp.where(extra_blocks >= 0, extra_blocks % per_block, 0)
    owned_here = owner_table == position
    ranked = jnp.cumsum(owned_here.astype(jnp.int32), axis=1) - 1
    slot_ids = jnp.arange(CAP, dtype=jnp.int32)
    chosen = owned_here[:, None, :] & (ranked[:, None, :] == slot_ids[None, :, None])
    send_valid = jnp.any(chosen, axis=2)
    send_index = jnp.sum(jnp.where(chosen, inside_table[:, None, :], 0), axis=2)
    key_value_subs = key_value.reshape(per_block, SUB * 2 * model_width)
    send_rows = jnp.take(key_value_subs, send_index.reshape(-1), axis=0).reshape(
        devices * CAP * SUB, 2 * model_width
    )
    extra_rows = lax.all_to_all(send_rows, "tm", split_axis=0, concat_axis=0, tiled=True)
    my_owners = lax.dynamic_index_in_dim(owner_table, position, 0, keepdims=False)
    owner_ids = jnp.arange(devices, dtype=jnp.int32)
    taken_count = jnp.sum((my_owners[None, :] == owner_ids[:, None]).astype(jnp.int32), axis=1)
    slot_live = taken_count[:, None] > slot_ids[None, :]
    extra_live = jnp.repeat(slot_live.reshape(-1), SUB)
    row_ids = jnp.arange(block_rows, dtype=jnp.int32)
    own_mask = row_ids[:, None] >= row_ids[None, :]
    partner_live = jnp.concatenate(
        [jnp.broadcast_to(position >= distance, (block_rows,)) for distance in distances]
    )
    far_live = jnp.concatenate([partner_live, extra_live])
    key_mask = jnp.concatenate(
        [own_mask, jnp.broadcast_to(far_live[None, :], (block_rows, far_live.shape[0]))], axis=1
    )
    all_keys = jnp.concatenate([key_value] + partner_blocks + [extra_rows], axis=0)

    def columns(array, group_index, offset):
        return array[
            :, offset + group_index * group_width : offset + (group_index + 1) * group_width
        ]

    mixed_parts, query_parts, key_parts, value_parts = ([], [], [], [])
    for group_index in range(group_count):
        query_part = columns(queries, group_index, 0)
        key_part = columns(all_keys, group_index, 0)
        value_part = columns(all_keys, group_index, model_width)
        weights, weights_low, mixed_part = forward_group(
            query_part, key_part, value_part, key_mask, scaling
        )
        mixed_parts.append(mixed_part)
        grads = backward_group(
            query_part,
            key_part,
            value_part,
            columns(grad_output, group_index, 0),
            mixed_part,
            weights,
            weights_low,
            scaling,
        )
        query_parts.append(grads[0])
        key_parts.append(grads[1])
        value_parts.append(grads[2])
    mixed_rows = jnp.concatenate(mixed_parts, axis=1)
    query_grad = jnp.concatenate(query_parts, axis=1).astype(jnp.bfloat16)
    grads_all = jnp.concatenate(
        [jnp.concatenate(key_parts, axis=1), jnp.concatenate(value_parts, axis=1)], axis=1
    )
    grad_total = grads_all[:block_rows]
    partner_terms = [
        grads_all[(1 + level) * block_rows : (2 + level) * block_rows]
        for level in range(len(distances))
    ]
    extra_terms = grads_all[(1 + len(distances)) * block_rows :]
    for level, distance in enumerate(distances):
        returned = from_behind(partner_terms[level].astype(jnp.bfloat16), "tm", -distance)
        grad_total = grad_total + returned.astype(jnp.float32)
    extra_back = lax.all_to_all(
        extra_terms.astype(jnp.bfloat16), "tm", split_axis=0, concat_axis=0, tiled=True
    )
    sub_ids = jnp.arange(per_block, dtype=jnp.int32)
    one_hot = (
        (send_index.reshape(-1)[None, :] == sub_ids[:, None]) & send_valid.reshape(-1)[None, :]
    ).astype(jnp.bfloat16)
    folded = jnp.dot(
        one_hot,
        extra_back.reshape(devices * CAP, SUB * 2 * model_width),
        preferred_element_type=jnp.float32,
    )
    grad_total = grad_total + folded.reshape(block_rows, 2 * model_width)
    key_grad = grad_total[:, :model_width].astype(jnp.bfloat16)
    value_grad = grad_total[:, model_width:].astype(jnp.bfloat16)
    return (mixed_rows, query_grad, key_grad, value_grad)


def nt(a, b):
    return lax.dot_general(a, b, (((1,), (1,)), ((), ())), preferred_element_type=jnp.float32)


def tn(a, b):
    return lax.dot_general(a, b, (((0,), (0,)), ((), ())), preferred_element_type=jnp.float32)


def nn(a, b):
    return lax.dot_general(a, b, (((1,), (0,)), ((), ())), preferred_element_type=jnp.float32)


def by_eights(x, op):
    acc = x[:8]
    for i in range(8, x.shape[0], 8):
        acc = op(acc, x[i : i + 8])
    return acc


def attention_kernel(blocks, rows, entries, table, kv, qd, oq, dkv, dacc, scores, xkv, acc, peak, total):
    levels = max(1, (blocks - 1).bit_length())
    width = 2 * HD
    tiles = rows // TILE
    scaling = 1.0 / math.sqrt(HD)
    extra_rows = entries * SUB
    dacc[...] = jnp.zeros_like(dacc)
    xkv[...] = jnp.zeros_like(xkv)
    lane = lax.broadcasted_iota(jnp.int32, (rows, width), 1)
    far = (1 + levels) * rows

    def one_block(step, carry):
        b = blocks - 1 - step
        start = pl.multiple_of(b * rows, rows)
        block = qd[pl.ds(start, rows), :]
        zero = jnp.zeros_like(block)
        q_part = jnp.where(lane < HD, block * CAST(scaling), zero)
        g_part = jnp.where(lane < HD, zero, block)
        live = jnp.int32(0)
        for e in range(entries):
            live = live + (table[b, e] >= 0).astype(jnp.int32)
        for e in range(entries):
            entry = table[b, e]

            @pl.when(entry >= 0)
            def _():
                xkv[e * SUB : (e + 1) * SUB, :] = kv[pl.ds(pl.multiple_of(entry * SUB, SUB), SUB), :]

        partners = jnp.int32(0)
        for level in range(levels):
            partners = partners + (b >= (1 << level)).astype(jnp.int32)
        extra_tiles = (live * SUB + TILE - 1) // TILE

        def partner_start(p):
            return pl.multiple_of((b - lax.shift_left(jnp.int32(1), p)) * rows, rows)

        def put_scores(keys, at, low, mask):
            s = nt(keys, q_part[low:])
            if mask is not None:
                s = jnp.where(mask(s.shape), s, LOWEST)
            scores[pl.ds(at, TILE), low:] = s
            peak[:, low:] = jnp.maximum(peak[:, low:], by_eights(s, jnp.maximum))

        peak[...] = jnp.full_like(peak, LOWEST)
        for t in range(tiles):
            put_scores(
                kv[pl.ds(start + t * TILE, TILE), :], t * TILE, t * TILE,
                lambda shape: lax.broadcasted_iota(jnp.int32, shape, 0) <= lax.broadcasted_iota(jnp.int32, shape, 1),
            )

        def partner_scores(p, c):
            base = partner_start(p)
            at = pl.multiple_of((1 + p) * rows, rows)
            for t in range(tiles):
                put_scores(kv[pl.ds(base + t * TILE, TILE), :], at + t * TILE, 0, None)
            return c

        lax.fori_loop(0, partners, partner_scores, 0)

        def extra_scores(t, c):
            at = pl.multiple_of(t * TILE, TILE)
            put_scores(
                xkv[pl.ds(at, TILE), :], far + at, 0,
                lambda shape: lax.broadcasted_iota(jnp.int32, shape, 0) + at < live * SUB,
            )
            return c

        lax.fori_loop(0, extra_tiles, extra_scores, 0)
        top = jnp.max(peak[...], axis=0, keepdims=True)

        total[...] = jnp.zeros_like(total)
        acc[...] = jnp.zeros_like(acc)

        def mix(keys, at, low):
            w = jnp.exp(scores[pl.ds(at, TILE), low:] - top[:, low:])
            total[:, low:] += by_eights(w, jnp.add)
            acc[HD:, low:] += tn(keys, w.astype(CAST))[HD:]

        for t in range(tiles):
            mix(kv[pl.ds(start + t * TILE, TILE), :], t * TILE, t * TILE)

        def partner_mix(p, c):
            base = partner_start(p)
            at = pl.multiple_of((1 + p) * rows, rows)
            for t in range(tiles):
                mix(kv[pl.ds(base + t * TILE, TILE), :], at + t * TILE, 0)
            return c

        lax.fori_loop(0, partners, partner_mix, 0)

        def extra_mix(t, c):
            at = pl.multiple_of(t * TILE, TILE)
            mix(xkv[pl.ds(at, TILE), :], far + at, 0)
            return c

        lax.fori_loop(0, extra_tiles, extra_mix, 0)
        weight_sum = jnp.sum(total[...], axis=0, keepdims=True)
        mixed = acc[HD:, :] / weight_sum
        acc[HD:, :] = mixed
        block_t = jnp.transpose(block.astype(jnp.float32))
        delta = jnp.sum(block_t[HD:] * mixed.astype(CAST).astype(jnp.float32), axis=0, keepdims=True)
        norm = top + jnp.log(weight_sum)

        def grads(keys, at, low):
            w = jnp.exp(scores[pl.ds(at, TILE), low:] - norm[:, low:])
            wg = nt(keys, g_part[low:])
            sg = (w * (wg - delta[:, low:])).astype(CAST)
            acc[:HD, low:] += tn(keys, sg)[:HD]
            return nn(sg, q_part[low:]) + nn(w.astype(CAST), g_part[low:])

        for t in range(tiles):
            at = start + t * TILE
            dacc[pl.ds(at, TILE), :] += grads(kv[pl.ds(at, TILE), :], t * TILE, t * TILE)

        def partner_grads(p, c):
            base = partner_start(p)
            at = pl.multiple_of((1 + p) * rows, rows)
            for t in range(tiles):
                dacc[pl.ds(base + t * TILE, TILE), :] += grads(kv[pl.ds(base + t * TILE, TILE), :], at + t * TILE, 0)
            return c

        lax.fori_loop(0, partners, partner_grads, 0)

        def extra_grads(t, c):
            at = pl.multiple_of(t * TILE, TILE)
            terms = grads(xkv[pl.ds(at, TILE), :], far + at, 0)
            for i in range(TILE // SUB):
                entry = table[b, t * (TILE // SUB) + i]

                @pl.when(entry >= 0)
                def _():
                    dacc[pl.ds(pl.multiple_of(entry * SUB, SUB), SUB), :] += terms[i * SUB : (i + 1) * SUB]
            return c

        lax.fori_loop(0, extra_tiles, extra_grads, 0)
        acc[:HD, :] = acc[:HD, :] * scaling
        oq[pl.ds(start, rows), :] = jnp.transpose(acc[...]).astype(CAST)
        dkv[pl.ds(start, rows), :] = dacc[pl.ds(start, rows), :].astype(CAST)
        return carry

    lax.fori_loop(0, blocks, one_block, 0)


def attention(table, kv, qd, rows):
    length, width = kv.shape
    blocks = length // rows
    entries = table.shape[1]
    levels = max(1, (blocks - 1).bit_length())
    whole = pl.BlockSpec(memory_space=pltpu.VMEM)
    return pl.pallas_call(
        functools.partial(attention_kernel, blocks, rows, entries),
        out_shape=(jax.ShapeDtypeStruct((length, width), CAST),) * 2,
        in_specs=[pl.BlockSpec(memory_space=pltpu.SMEM), whole, whole],
        out_specs=(whole, whole),
        scratch_shapes=[
            pltpu.VMEM((length, width), jnp.float32),
            pltpu.VMEM(((1 + levels) * rows + entries * SUB, rows), jnp.float32),
            pltpu.VMEM((entries * SUB, width), CAST),
            pltpu.VMEM((width, rows), jnp.float32),
            pltpu.VMEM((8, rows), jnp.float32),
            pltpu.VMEM((8, rows), jnp.float32),
        ],
        compiler_params=pltpu.CompilerParams(vmem_limit_bytes=48 * 1024 * 1024),
    )(table, kv, qd)


def swap(x):
    return jnp.concatenate([x[:, HD:], x[:, :HD]], axis=1)

def interleave(first, second):
    lane = lax.broadcasted_iota(jnp.int32, first.shape, 1)
    return jnp.where(lane < HD, first, swap(second)), jnp.where(lane < HD, swap(first), second)

def pack_kernel(heads, q, k, v, g, out):
    for pair in range(heads // 2):
        lanes = slice(pair * 2 * HD, (pair + 1) * 2 * HD)
        kv = interleave(k[:, lanes], v[:, lanes])
        qg = interleave(q[:, lanes], g[:, lanes])
        for i in range(2):
            out[2 * pair + i, :, : 2 * HD] = kv[i]
            out[2 * pair + i, :, 2 * HD :] = qg[i]

def unpack_kernel(heads, x, o, dq, dk, dv):
    for pair in range(heads // 2):
        lanes = slice(pair * 2 * HD, (pair + 1) * 2 * HD)
        even, odd = x[2 * pair], x[2 * pair + 1]
        dq[:, lanes], o[:, lanes] = interleave(even[:, : 2 * HD], odd[:, : 2 * HD])
        dk[:, lanes], dv[:, lanes] = interleave(even[:, 2 * HD :], odd[:, 2 * HD :])

def pack(q, k, v, g):
    rows, width = q.shape
    heads = width // HD
    whole = pl.BlockSpec(memory_space=pltpu.VMEM)
    return pl.pallas_call(functools.partial(pack_kernel, heads),
        out_shape=jax.ShapeDtypeStruct((heads, rows, 4 * HD), q.dtype),
        in_specs=[whole]*4, out_specs=whole)(q, k, v, g)

def unpack(x):
    heads, rows, _ = x.shape
    whole = pl.BlockSpec(memory_space=pltpu.VMEM)
    return pl.pallas_call(functools.partial(unpack_kernel, heads),
        out_shape=(jax.ShapeDtypeStruct((rows, heads * HD), x.dtype),) * 4,
        in_specs=[whole], out_specs=(whole,)*4)(x)


def head_plan(queries, key_rows, value_rows, grad_output, extra_blocks):
    rows = queries.shape[0]
    heads = queries.shape[1] // HD
    packed = pack(queries, key_rows, value_rows, grad_output)
    gathered = lax.all_to_all(packed, "tm", split_axis=0, concat_axis=0, tiled=True)
    gathered = gathered.reshape(heads * rows, 4 * HD)
    oq, dkv = attention(extra_blocks, gathered[:, : 2 * HD], gathered[:, 2 * HD :], rows)
    both = jnp.concatenate([oq, dkv], axis=1).reshape(heads, rows, 4 * HD)
    back = lax.all_to_all(both, "tm", split_axis=0, concat_axis=0, tiled=True)
    return unpack(back)


def local(queries, key_rows, value_rows, grad_output, extra_blocks):
    if lax.axis_size("tm") == queries.shape[1] // HD:
        return head_plan(queries, key_rows, value_rows, grad_output, extra_blocks)
    return block_plan(queries, key_rows, value_rows, grad_output, extra_blocks)


def solution(mesh):
    placed = (
        P(("member", "tm"), None),
        P(("member", "tm"), None),
        P(("member", "tm"), None),
        P(("member", "tm"), None),
        P("member", None),
    )
    return jax.shard_map(
        local,
        mesh=mesh,
        in_specs=placed,
        out_specs=(
            P(("member", "tm"), None),
            P(("member", "tm"), None),
            P(("member", "tm"), None),
            P(("member", "tm"), None),
        ),
        check_vma=False,
    )
```

```python
import functools
import math

import jax
import jax.numpy as jnp
from jax import lax
from jax.experimental import pallas as pl
from jax.experimental.pallas import tpu as pltpu
from jax.sharding import PartitionSpec as P

HD = 64
HG = 2
SUB = 16
CAP = 2
TILE = 256
LOWEST = -1e30
CAST = jnp.bfloat16


very_negative = -1e30


def from_behind(value, axis, by):
    peers = lax.axis_size(axis)
    pairs = [(i, i + by) for i in range(peers) if 0 <= i + by < peers]
    return lax.ppermute(value, axis, pairs)


def split_heads(values):
    return values.reshape(values.shape[0], values.shape[1] // HD, HD)


def forward_group(query_part, key_part, value_part, key_mask, scaling):
    scores = (
        jnp.einsum(
            "qhd,khd->hqk",
            split_heads(query_part),
            split_heads(key_part),
            preferred_element_type=jnp.float32,
        )
        * scaling
    )
    scores = jnp.where(key_mask[None], scores, very_negative)
    weights = jax.nn.softmax(scores, axis=-1)
    weights_low = weights.astype(jnp.bfloat16)
    mixed_heads = jnp.einsum(
        "hqk,khd->qhd", weights_low, split_heads(value_part), preferred_element_type=jnp.float32
    )
    mixed_part = mixed_heads.reshape(query_part.shape).astype(jnp.bfloat16)
    return (weights, weights_low, mixed_part)


def backward_group(
    query_part, key_part, value_part, grad_part, mixed_part, weights, weights_low, scaling
):
    grad_heads = split_heads(grad_part)
    row_delta = jnp.sum(
        grad_heads.astype(jnp.float32) * split_heads(mixed_part).astype(jnp.float32), axis=-1
    )
    row_delta = jnp.transpose(row_delta)[:, :, None]
    weight_grads = jnp.einsum(
        "qhd,khd->hqk", grad_heads, split_heads(value_part), preferred_element_type=jnp.float32
    )
    score_grads = (weights * (weight_grads - row_delta)).astype(jnp.bfloat16)
    query_grads = (
        jnp.einsum(
            "hqk,khd->qhd", score_grads, split_heads(key_part), preferred_element_type=jnp.float32
        )
        * scaling
    )
    key_grads = (
        jnp.einsum(
            "hqk,qhd->khd", score_grads, split_heads(query_part), preferred_element_type=jnp.float32
        )
        * scaling
    )
    value_grads = jnp.einsum(
        "hqk,qhd->khd", weights_low, grad_heads, preferred_element_type=jnp.float32
    )
    return (
        query_grads.reshape(query_part.shape),
        key_grads.reshape(key_part.shape),
        value_grads.reshape(key_part.shape),
    )


def block_plan(queries, key_rows, value_rows, grad_output, extra_blocks):
    devices = lax.axis_size("tm")
    position = lax.axis_index("tm")
    block_rows = queries.shape[0]
    model_width = queries.shape[1]
    per_block = block_rows // SUB
    group_width = HG * HD
    group_count = model_width // group_width
    scaling = 1.0 / math.sqrt(HD)
    distances = []
    reach = 1
    while reach < devices:
        distances.append(reach)
        reach = reach * 2
    key_value = jnp.concatenate([key_rows, value_rows], axis=1)
    partner_blocks = [from_behind(key_value, "tm", distance) for distance in distances]
    owner_table = jnp.where(extra_blocks >= 0, extra_blocks // per_block, -1)
    inside_table = jnp.where(extra_blocks >= 0, extra_blocks % per_block, 0)
    owned_here = owner_table == position
    ranked = jnp.cumsum(owned_here.astype(jnp.int32), axis=1) - 1
    slot_ids = jnp.arange(CAP, dtype=jnp.int32)
    chosen = owned_here[:, None, :] & (ranked[:, None, :] == slot_ids[None, :, None])
    send_valid = jnp.any(chosen, axis=2)
    send_index = jnp.sum(jnp.where(chosen, inside_table[:, None, :], 0), axis=2)
    key_value_subs = key_value.reshape(per_block, SUB * 2 * model_width)
    send_rows = jnp.take(key_value_subs, send_index.reshape(-1), axis=0).reshape(
        devices * CAP * SUB, 2 * model_width
    )
    extra_rows = lax.all_to_all(send_rows, "tm", split_axis=0, concat_axis=0, tiled=True)
    my_owners = lax.dynamic_index_in_dim(owner_table, position, 0, keepdims=False)
    owner_ids = jnp.arange(devices, dtype=jnp.int32)
    taken_count = jnp.sum((my_owners[None, :] == owner_ids[:, None]).astype(jnp.int32), axis=1)
    slot_live = taken_count[:, None] > slot_ids[None, :]
    extra_live = jnp.repeat(slot_live.reshape(-1), SUB)
    row_ids = jnp.arange(block_rows, dtype=jnp.int32)
    own_mask = row_ids[:, None] >= row_ids[None, :]
    partner_live = jnp.concatenate(
        [jnp.broadcast_to(position >= distance, (block_rows,)) for distance in distances]
    )
    far_live = jnp.concatenate([partner_live, extra_live])
    key_mask = jnp.concatenate(
        [own_mask, jnp.broadcast_to(far_live[None, :], (block_rows, far_live.shape[0]))], axis=1
    )
    all_keys = jnp.concatenate([key_value] + partner_blocks + [extra_rows], axis=0)

    def columns(array, group_index, offset):
        return array[
            :, offset + group_index * group_width : offset + (group_index + 1) * group_width
        ]

    mixed_parts, query_parts, key_parts, value_parts = ([], [], [], [])
    for group_index in range(group_count):
        query_part = columns(queries, group_index, 0)
        key_part = columns(all_keys, group_index, 0)
        value_part = columns(all_keys, group_index, model_width)
        weights, weights_low, mixed_part = forward_group(
            query_part, key_part, value_part, key_mask, scaling
        )
        mixed_parts.append(mixed_part)
        grads = backward_group(
            query_part,
            key_part,
            value_part,
            columns(grad_output, group_index, 0),
            mixed_part,
            weights,
            weights_low,
            scaling,
        )
        query_parts.append(grads[0])
        key_parts.append(grads[1])
        value_parts.append(grads[2])
    mixed_rows = jnp.concatenate(mixed_parts, axis=1)
    query_grad = jnp.concatenate(query_parts, axis=1).astype(jnp.bfloat16)
    grads_all = jnp.concatenate(
        [jnp.concatenate(key_parts, axis=1), jnp.concatenate(value_parts, axis=1)], axis=1
    )
    grad_total = grads_all[:block_rows]
    partner_terms = [
        grads_all[(1 + level) * block_rows : (2 + level) * block_rows]
        for level in range(len(distances))
    ]
    extra_terms = grads_all[(1 + len(distances)) * block_rows :]
    for level, distance in enumerate(distances):
        returned = from_behind(partner_terms[level].astype(jnp.bfloat16), "tm", -distance)
        grad_total = grad_total + returned.astype(jnp.float32)
    extra_back = lax.all_to_all(
        extra_terms.astype(jnp.bfloat16), "tm", split_axis=0, concat_axis=0, tiled=True
    )
    sub_ids = jnp.arange(per_block, dtype=jnp.int32)
    one_hot = (
        (send_index.reshape(-1)[None, :] == sub_ids[:, None]) & send_valid.reshape(-1)[None, :]
    ).astype(jnp.bfloat16)
    folded = jnp.dot(
        one_hot,
        extra_back.reshape(devices * CAP, SUB * 2 * model_width),
        preferred_element_type=jnp.float32,
    )
    grad_total = grad_total + folded.reshape(block_rows, 2 * model_width)
    key_grad = grad_total[:, :model_width].astype(jnp.bfloat16)
    value_grad = grad_total[:, model_width:].astype(jnp.bfloat16)
    return (mixed_rows, query_grad, key_grad, value_grad)


def nn(a, b):
    return lax.dot_general(a, b, (((1,), (0,)), ((), ())), preferred_element_type=jnp.float32)


def tn(a, b):
    return lax.dot_general(a, b, (((0,), (0,)), ((), ())), preferred_element_type=jnp.float32)


def by_eights(x, op):
    parts = [x[i : i + 8] for i in range(0, x.shape[0], 8)]
    while len(parts) > 1:
        parts = [op(*parts[i : i + 2]) if i + 1 < len(parts) else parts[i] for i in range(0, len(parts), 2)]
    return parts[0]


def widen(x, low, fill):
    if low == 0:
        return x
    return jnp.concatenate([jnp.full((x.shape[0], low), fill, x.dtype), x], axis=1)


def attention_kernel(blocks, rows, entries, table, kv, qd, oq, dkv, dacc, scores, xkv, terms):
    levels = (blocks - 1).bit_length()
    width = 2 * HD
    scaling = 1.0 / math.sqrt(HD)
    extra_rows = entries * SUB
    dacc[...] = jnp.zeros_like(dacc)

    def one_block(partners, b):
        start = pl.multiple_of(b * rows, rows)
        block = qd[pl.ds(start, rows), :]
        lane = lax.broadcasted_iota(jnp.int32, (rows, width), 1)
        zero = jnp.zeros_like(block)
        q_part = jnp.where(lane < HD, block * CAST(scaling), zero)
        g_part = jnp.where(lane < HD, zero, block)
        block_t = jnp.transpose(block.astype(jnp.float32))
        row_t = lax.broadcasted_iota(jnp.int32, (width, rows), 0)
        q_t = jnp.where(row_t < HD, block_t * scaling, 0.0).astype(CAST)
        g_t = jnp.where(row_t < HD, 0.0, block_t).astype(CAST)

        chunks = []
        for t in range(0, rows, TILE):
            chunks.append((kv, start + t, t, TILE, t, "own"))
        for p in range(partners):
            chunks.append((kv, pl.multiple_of((b - (1 << p)) * rows, rows), (1 + p) * rows, rows, 0, None))
        if partners:
            live = jnp.int32(0)
            for e in range(entries):
                entry = table[b, e]
                live = live + (entry >= 0).astype(jnp.int32)
                at = pl.multiple_of(jnp.maximum(entry, 0) * SUB, SUB)
                xkv[e * SUB : (e + 1) * SUB, :] = kv[pl.ds(at, SUB), :]
            chunks.append((xkv, 0, (1 + partners) * rows, extra_rows, 0, "extra"))

        peak = jnp.full((8, rows), LOWEST, jnp.float32)
        for ref, first, at, count, low, mask in chunks:
            s = nn(ref[pl.ds(first, count), :], q_t[:, low:])
            if mask == "own":
                s = jnp.where(
                    lax.broadcasted_iota(jnp.int32, s.shape, 0) <= lax.broadcasted_iota(jnp.int32, s.shape, 1), s, LOWEST
                )
            if mask == "extra":
                s = jnp.where(lax.broadcasted_iota(jnp.int32, s.shape, 0) < live * SUB, s, LOWEST)
            scores[at : at + count, low:] = s
            peak = jnp.maximum(peak, widen(by_eights(s, jnp.maximum), low, LOWEST))
        top = jnp.max(peak, axis=0, keepdims=True)

        total = jnp.zeros((8, rows), jnp.float32)
        mixed = jnp.zeros((HD, rows), jnp.float32)
        for ref, first, at, count, low, mask in chunks:
            w = jnp.exp(scores[at : at + count, low:] - top[:, low:])
            total = total + widen(by_eights(w, jnp.add), low, 0.0)
            mixed = mixed + widen(tn(ref[pl.ds(first, count), :], w.astype(CAST))[HD:], low, 0.0)
        weight_sum = jnp.sum(total, axis=0, keepdims=True)
        mixed = mixed / weight_sum
        delta = jnp.sum(block_t[HD:] * mixed.astype(CAST).astype(jnp.float32), axis=0, keepdims=True)
        norm = top + jnp.log(weight_sum)

        query_grad = jnp.zeros((HD, rows), jnp.float32)
        for ref, first, at, count, low, mask in chunks:
            keys = ref[pl.ds(first, count), :]
            w = jnp.exp(scores[at : at + count, low:] - norm[:, low:])
            sg = (w * (nn(keys, g_t[:, low:]) - delta[:, low:])).astype(CAST)
            query_grad = query_grad + widen(tn(keys, sg)[:HD], low, 0.0)
            part = nn(sg, q_part[low:]) + nn(w.astype(CAST), g_part[low:])
            if mask == "extra":
                terms[...] = part
            else:
                dacc[pl.ds(first, count), :] += part
        if partners:
            for e in range(entries):
                at = pl.multiple_of(jnp.maximum(table[b, e], 0) * SUB, SUB)
                dacc[pl.ds(at, SUB), :] += terms[e * SUB : (e + 1) * SUB, :]
        oq[pl.ds(start, rows), :] = jnp.transpose(jnp.concatenate([query_grad * scaling, mixed], axis=0)).astype(CAST)
        dkv[pl.ds(start, rows), :] = dacc[pl.ds(start, rows), :].astype(CAST)

    for partners in range(levels, -1, -1):
        low = (1 << partners) >> 1
        high = min(1 << partners, blocks)

        def step(i, carry, partners=partners, high=high):
            one_block(partners, high - 1 - i)
            return carry

        if high - low > 1:
            lax.fori_loop(0, high - low, step, 0)
        else:
            one_block(partners, jnp.int32(low))


def attention(table, kv, qd, rows):
    length, width = kv.shape
    blocks = length // rows
    entries = table.shape[1]
    levels = (blocks - 1).bit_length()
    whole = pl.BlockSpec(memory_space=pltpu.VMEM)
    return pl.pallas_call(
        functools.partial(attention_kernel, blocks, rows, entries),
        out_shape=(jax.ShapeDtypeStruct((length, width), CAST),) * 2,
        in_specs=[pl.BlockSpec(memory_space=pltpu.SMEM), whole, whole],
        out_specs=(whole, whole),
        scratch_shapes=[
            pltpu.VMEM((length, width), jnp.float32),
            pltpu.VMEM(((1 + levels) * rows + entries * SUB, rows), jnp.float32),
            pltpu.VMEM((entries * SUB, width), CAST),
            pltpu.VMEM((entries * SUB, width), jnp.float32),
        ],
        compiler_params=pltpu.CompilerParams(vmem_limit_bytes=56 * 1024 * 1024),
    )(table, kv, qd)


def swap(x):
    return jnp.concatenate([x[:, HD:], x[:, :HD]], axis=1)

def interleave(first, second):
    lane = lax.broadcasted_iota(jnp.int32, first.shape, 1)
    return jnp.where(lane < HD, first, swap(second)), jnp.where(lane < HD, swap(first), second)

def pack_kernel(heads, q, k, v, g, out):
    for pair in range(heads // 2):
        lanes = slice(pair * 2 * HD, (pair + 1) * 2 * HD)
        kv = interleave(k[:, lanes], v[:, lanes])
        qg = interleave(q[:, lanes], g[:, lanes])
        for i in range(2):
            out[2 * pair + i, :, : 2 * HD] = kv[i]
            out[2 * pair + i, :, 2 * HD :] = qg[i]

def unpack_kernel(heads, x, o, dq, dk, dv):
    for pair in range(heads // 2):
        lanes = slice(pair * 2 * HD, (pair + 1) * 2 * HD)
        even, odd = x[2 * pair], x[2 * pair + 1]
        dq[:, lanes], o[:, lanes] = interleave(even[:, : 2 * HD], odd[:, : 2 * HD])
        dk[:, lanes], dv[:, lanes] = interleave(even[:, 2 * HD :], odd[:, 2 * HD :])

def pack(q, k, v, g):
    rows, width = q.shape
    heads = width // HD
    whole = pl.BlockSpec(memory_space=pltpu.VMEM)
    return pl.pallas_call(functools.partial(pack_kernel, heads),
        out_shape=jax.ShapeDtypeStruct((heads, rows, 4 * HD), q.dtype),
        in_specs=[whole]*4, out_specs=whole)(q, k, v, g)

def unpack(x):
    heads, rows, _ = x.shape
    whole = pl.BlockSpec(memory_space=pltpu.VMEM)
    return pl.pallas_call(functools.partial(unpack_kernel, heads),
        out_shape=(jax.ShapeDtypeStruct((rows, heads * HD), x.dtype),) * 4,
        in_specs=[whole], out_specs=(whole,)*4)(x)


def head_plan(queries, key_rows, value_rows, grad_output, extra_blocks):
    rows = queries.shape[0]
    heads = queries.shape[1] // HD
    packed = pack(queries, key_rows, value_rows, grad_output)
    gathered = lax.all_to_all(packed, "tm", split_axis=0, concat_axis=0, tiled=True)
    gathered = gathered.reshape(heads * rows, 4 * HD)
    oq, dkv = attention(extra_blocks, gathered[:, : 2 * HD], gathered[:, 2 * HD :], rows)
    both = jnp.concatenate([oq, dkv], axis=1).reshape(heads, rows, 4 * HD)
    back = lax.all_to_all(both, "tm", split_axis=0, concat_axis=0, tiled=True)
    return unpack(back)


def local(queries, key_rows, value_rows, grad_output, extra_blocks):
    if lax.axis_size("tm") == queries.shape[1] // HD:
        return head_plan(queries, key_rows, value_rows, grad_output, extra_blocks)
    return block_plan(queries, key_rows, value_rows, grad_output, extra_blocks)


def solution(mesh):
    placed = (
        P(("member", "tm"), None),
        P(("member", "tm"), None),
        P(("member", "tm"), None),
        P(("member", "tm"), None),
        P("member", None),
    )
    return jax.shard_map(
        local,
        mesh=mesh,
        in_specs=placed,
        out_specs=(
            P(("member", "tm"), None),
            P(("member", "tm"), None),
            P(("member", "tm"), None),
            P(("member", "tm"), None),
        ),
        check_vma=False,
    )
```

```python
import functools
import math

import jax
import jax.numpy as jnp
from jax import lax
from jax.experimental import pallas as pl
from jax.experimental.pallas import tpu as pltpu
from jax.sharding import PartitionSpec as P

HD = 64
HG = 2
SUB = 16
CAP = 2
TILE = 256
LOWEST = -1e30
CAST = jnp.bfloat16
TOGETHER = 2


very_negative = -1e30


def from_behind(value, axis, by):
    peers = lax.axis_size(axis)
    pairs = [(i, i + by) for i in range(peers) if 0 <= i + by < peers]
    return lax.ppermute(value, axis, pairs)


def split_heads(values):
    return values.reshape(values.shape[0], values.shape[1] // HD, HD)


def forward_group(query_part, key_part, value_part, key_mask, scaling):
    scores = (
        jnp.einsum(
            "qhd,khd->hqk",
            split_heads(query_part),
            split_heads(key_part),
            preferred_element_type=jnp.float32,
        )
        * scaling
    )
    scores = jnp.where(key_mask[None], scores, very_negative)
    weights = jax.nn.softmax(scores, axis=-1)
    weights_low = weights.astype(jnp.bfloat16)
    mixed_heads = jnp.einsum(
        "hqk,khd->qhd", weights_low, split_heads(value_part), preferred_element_type=jnp.float32
    )
    mixed_part = mixed_heads.reshape(query_part.shape).astype(jnp.bfloat16)
    return (weights, weights_low, mixed_part)


def backward_group(
    query_part, key_part, value_part, grad_part, mixed_part, weights, weights_low, scaling
):
    grad_heads = split_heads(grad_part)
    row_delta = jnp.sum(
        grad_heads.astype(jnp.float32) * split_heads(mixed_part).astype(jnp.float32), axis=-1
    )
    row_delta = jnp.transpose(row_delta)[:, :, None]
    weight_grads = jnp.einsum(
        "qhd,khd->hqk", grad_heads, split_heads(value_part), preferred_element_type=jnp.float32
    )
    score_grads = (weights * (weight_grads - row_delta)).astype(jnp.bfloat16)
    query_grads = (
        jnp.einsum(
            "hqk,khd->qhd", score_grads, split_heads(key_part), preferred_element_type=jnp.float32
        )
        * scaling
    )
    key_grads = (
        jnp.einsum(
            "hqk,qhd->khd", score_grads, split_heads(query_part), preferred_element_type=jnp.float32
        )
        * scaling
    )
    value_grads = jnp.einsum(
        "hqk,qhd->khd", weights_low, grad_heads, preferred_element_type=jnp.float32
    )
    return (
        query_grads.reshape(query_part.shape),
        key_grads.reshape(key_part.shape),
        value_grads.reshape(key_part.shape),
    )


def block_plan(queries, key_rows, value_rows, grad_output, extra_blocks):
    devices = lax.axis_size("tm")
    position = lax.axis_index("tm")
    block_rows = queries.shape[0]
    model_width = queries.shape[1]
    per_block = block_rows // SUB
    group_width = HG * HD
    group_count = model_width // group_width
    scaling = 1.0 / math.sqrt(HD)
    distances = []
    reach = 1
    while reach < devices:
        distances.append(reach)
        reach = reach * 2
    key_value = jnp.concatenate([key_rows, value_rows], axis=1)
    partner_blocks = [from_behind(key_value, "tm", distance) for distance in distances]
    owner_table = jnp.where(extra_blocks >= 0, extra_blocks // per_block, -1)
    inside_table = jnp.where(extra_blocks >= 0, extra_blocks % per_block, 0)
    owned_here = owner_table == position
    ranked = jnp.cumsum(owned_here.astype(jnp.int32), axis=1) - 1
    slot_ids = jnp.arange(CAP, dtype=jnp.int32)
    chosen = owned_here[:, None, :] & (ranked[:, None, :] == slot_ids[None, :, None])
    send_valid = jnp.any(chosen, axis=2)
    send_index = jnp.sum(jnp.where(chosen, inside_table[:, None, :], 0), axis=2)
    key_value_subs = key_value.reshape(per_block, SUB * 2 * model_width)
    send_rows = jnp.take(key_value_subs, send_index.reshape(-1), axis=0).reshape(
        devices * CAP * SUB, 2 * model_width
    )
    extra_rows = lax.all_to_all(send_rows, "tm", split_axis=0, concat_axis=0, tiled=True)
    my_owners = lax.dynamic_index_in_dim(owner_table, position, 0, keepdims=False)
    owner_ids = jnp.arange(devices, dtype=jnp.int32)
    taken_count = jnp.sum((my_owners[None, :] == owner_ids[:, None]).astype(jnp.int32), axis=1)
    slot_live = taken_count[:, None] > slot_ids[None, :]
    extra_live = jnp.repeat(slot_live.reshape(-1), SUB)
    row_ids = jnp.arange(block_rows, dtype=jnp.int32)
    own_mask = row_ids[:, None] >= row_ids[None, :]
    partner_live = jnp.concatenate(
        [jnp.broadcast_to(position >= distance, (block_rows,)) for distance in distances]
    )
    far_live = jnp.concatenate([partner_live, extra_live])
    key_mask = jnp.concatenate(
        [own_mask, jnp.broadcast_to(far_live[None, :], (block_rows, far_live.shape[0]))], axis=1
    )
    all_keys = jnp.concatenate([key_value] + partner_blocks + [extra_rows], axis=0)

    def columns(array, group_index, offset):
        return array[
            :, offset + group_index * group_width : offset + (group_index + 1) * group_width
        ]

    mixed_parts, query_parts, key_parts, value_parts = ([], [], [], [])
    for group_index in range(group_count):
        query_part = columns(queries, group_index, 0)
        key_part = columns(all_keys, group_index, 0)
        value_part = columns(all_keys, group_index, model_width)
        weights, weights_low, mixed_part = forward_group(
            query_part, key_part, value_part, key_mask, scaling
        )
        mixed_parts.append(mixed_part)
        grads = backward_group(
            query_part,
            key_part,
            value_part,
            columns(grad_output, group_index, 0),
            mixed_part,
            weights,
            weights_low,
            scaling,
        )
        query_parts.append(grads[0])
        key_parts.append(grads[1])
        value_parts.append(grads[2])
    mixed_rows = jnp.concatenate(mixed_parts, axis=1)
    query_grad = jnp.concatenate(query_parts, axis=1).astype(jnp.bfloat16)
    grads_all = jnp.concatenate(
        [jnp.concatenate(key_parts, axis=1), jnp.concatenate(value_parts, axis=1)], axis=1
    )
    grad_total = grads_all[:block_rows]
    partner_terms = [
        grads_all[(1 + level) * block_rows : (2 + level) * block_rows]
        for level in range(len(distances))
    ]
    extra_terms = grads_all[(1 + len(distances)) * block_rows :]
    for level, distance in enumerate(distances):
        returned = from_behind(partner_terms[level].astype(jnp.bfloat16), "tm", -distance)
        grad_total = grad_total + returned.astype(jnp.float32)
    extra_back = lax.all_to_all(
        extra_terms.astype(jnp.bfloat16), "tm", split_axis=0, concat_axis=0, tiled=True
    )
    sub_ids = jnp.arange(per_block, dtype=jnp.int32)
    one_hot = (
        (send_index.reshape(-1)[None, :] == sub_ids[:, None]) & send_valid.reshape(-1)[None, :]
    ).astype(jnp.bfloat16)
    folded = jnp.dot(
        one_hot,
        extra_back.reshape(devices * CAP, SUB * 2 * model_width),
        preferred_element_type=jnp.float32,
    )
    grad_total = grad_total + folded.reshape(block_rows, 2 * model_width)
    key_grad = grad_total[:, :model_width].astype(jnp.bfloat16)
    value_grad = grad_total[:, model_width:].astype(jnp.bfloat16)
    return (mixed_rows, query_grad, key_grad, value_grad)


def nn(a, b):
    return lax.dot_general(a, b, (((1,), (0,)), ((), ())), preferred_element_type=jnp.float32)


def tn(a, b):
    return lax.dot_general(a, b, (((0,), (0,)), ((), ())), preferred_element_type=jnp.float32)


def by_eights(x, op):
    parts = [x[i : i + 8] for i in range(0, x.shape[0], 8)]
    while len(parts) > 1:
        parts = [op(*parts[i : i + 2]) if i + 1 < len(parts) else parts[i] for i in range(0, len(parts), 2)]
    return parts[0]


class Block:
    def __init__(self, b, partners, rows, first_query, queries, table, kv, block, scores, gathered, dacc):
        self.kv, self.scores, self.gathered, self.dacc, self.table, self.b = kv, scores, gathered, dacc, table, b
        self.queries = queries
        entries = table.shape[1]
        width = 2 * HD
        scaling = 1.0 / math.sqrt(HD)
        lane = lax.broadcasted_iota(jnp.int32, block.shape, 1)
        zero = jnp.zeros_like(block)
        self.q_part = jnp.where(lane < HD, block * CAST(scaling), zero)
        self.g_part = jnp.where(lane < HD, zero, block)
        self.block_t = jnp.transpose(block.astype(jnp.float32))
        row_t = lax.broadcasted_iota(jnp.int32, (width, queries), 0)
        self.q_t = jnp.where(row_t < HD, self.block_t * scaling, 0.0).astype(CAST)
        self.g_t = jnp.where(row_t < HD, 0.0, self.block_t).astype(CAST)
        self.chunks = []
        if first_query:
            self.chunks.append((b, 0, first_query, "all"))
        self.chunks.append((b, first_query, queries, "own"))
        for p in range(partners):
            self.chunks.append((b - (1 << p), 0, rows, "all"))
        self.extra_places = []
        if partners:
            self.live = jnp.int32(0)
            for e in range(entries):
                entry = table[b, e]
                self.live = self.live + (entry >= 0).astype(jnp.int32)
                entry = jnp.maximum(entry, 0)
                place = (entry // (rows // SUB), pl.multiple_of(entry % (rows // SUB) * SUB, SUB))
                self.extra_places.append(place)
                gathered[e * SUB : (e + 1) * SUB, :] = kv[place[0], pl.ds(place[1], SUB), :]
            self.chunks.append((None, 0, entries * SUB, "extra"))
        self.places = []
        at = 0
        for chunk in self.chunks:
            self.places.append(slice(at, at + chunk[2]))
            at += chunk[2]

    def keys(self, chunk):
        block, first, count, kind = chunk
        if kind == "extra":
            return self.gathered[...]
        return self.kv[block, first : first + count, :]

    def score(self):
        peak = jnp.full((8, self.queries), LOWEST, jnp.float32)
        for chunk, place in zip(self.chunks, self.places):
            s = nn(self.keys(chunk), self.q_t)
            row = lax.broadcasted_iota(jnp.int32, s.shape, 0)
            if chunk[3] == "own":
                s = jnp.where(row <= lax.broadcasted_iota(jnp.int32, s.shape, 1), s, LOWEST)
            if chunk[3] == "extra":
                s = jnp.where(row < self.live * SUB, s, LOWEST)
            self.scores[place, :] = s
            peak = jnp.maximum(peak, by_eights(s, jnp.maximum))
        self.top = jnp.max(peak, axis=0, keepdims=True)

    def mix(self):
        total = jnp.zeros((8, self.queries), jnp.float32)
        mixed = jnp.zeros((HD, self.queries), jnp.float32)
        for chunk, place in zip(self.chunks, self.places):
            w = jnp.exp(self.scores[place, :] - self.top)
            total = total + by_eights(w, jnp.add)
            mixed = mixed + tn(self.keys(chunk), w.astype(CAST))[HD:]
        total = jnp.sum(total, axis=0, keepdims=True)
        self.mixed = mixed / total
        low = self.mixed.astype(CAST).astype(jnp.float32)
        self.delta = jnp.sum(self.block_t[HD:] * low, axis=0, keepdims=True)
        self.norm = self.top + jnp.log(total)

    def grads(self):
        query_grad = jnp.zeros((HD, self.queries), jnp.float32)
        for chunk, place in zip(self.chunks, self.places):
            keys = self.keys(chunk)
            w = jnp.exp(self.scores[place, :] - self.norm)
            sg = (w * (nn(keys, self.g_t) - self.delta)).astype(CAST)
            query_grad = query_grad + tn(keys, sg)[:HD]
            part = nn(sg, self.q_part) + nn(w.astype(CAST), self.g_part)
            block, first, count, kind = chunk
            if kind == "extra":
                for e, (owner, at) in enumerate(self.extra_places):
                    self.dacc[owner, pl.ds(at, SUB), :] += part[e * SUB : (e + 1) * SUB]
            else:
                self.dacc[block, first : first + count, :] += part
        return jnp.transpose(jnp.concatenate([query_grad * (1.0 / math.sqrt(HD)), self.mixed], axis=0)).astype(CAST)


def attention_kernel(rows, first_query, queries, query_at, last, together, *refs):
    if first_query:
        table, kv, qd, before, out, dacc, scores, gathered = refs
        dacc[...] = before[...]
    else:
        table, kv, qd, out, dacc, scores, gathered = refs
        dacc[...] = jnp.zeros_like(dacc)
    blocks = kv.shape[0]
    levels = (blocks - 1).bit_length()
    out_at = rows if last else 0

    def run(partners, ids):
        work = [
            Block(b, partners, rows, first_query, queries, table, kv, qd[b, query_at : query_at + queries, :],
                  scores.at[i], gathered.at[i], dacc)
            for i, b in enumerate(ids)
        ]
        for w in work:
            w.score()
        for w in work:
            w.mix()
        for w in work:
            out[w.b, out_at : out_at + queries, :] = w.grads()
        if last:
            for w in work:
                out[w.b, :rows, :] = dacc[w.b].astype(CAST)

    for partners in range(levels, -1, -1):
        low = (1 << partners) >> 1
        high = min(1 << partners, blocks)
        group = math.gcd(together, high - low)

        def step(i, carry, partners=partners, high=high, group=group):
            run(partners, [high - 1 - i * group - j for j in range(group)])
            return carry

        if high - low > group:
            lax.fori_loop(0, (high - low) // group, step, 0)
        else:
            run(partners, [jnp.int32(high - 1 - j) for j in range(group)])


def attention(table, kv, qd, before, rows, first_query, queries, query_at, last, together=None):
    together = TOGETHER if together is None else together
    blocks, _, width = kv.shape
    entries = table.shape[1]
    levels = (blocks - 1).bit_length()
    whole = pl.BlockSpec(memory_space=pltpu.VMEM)
    sums = jax.ShapeDtypeStruct((blocks, rows, width), jnp.float32)
    if last:
        out_shape = jax.ShapeDtypeStruct((blocks, rows + queries, width), CAST)
        out_specs = whole
    else:
        out_shape = (jax.ShapeDtypeStruct((blocks, queries, width), CAST), sums)
        out_specs = (whole, whole)
    inputs = (table, kv, qd) + ((before,) if first_query else ())
    list_rows = first_query + queries + levels * rows + entries * SUB
    scratch = [
        pltpu.VMEM((together, list_rows, queries), jnp.float32),
        pltpu.VMEM((together, entries * SUB, width), CAST),
    ]
    if last:
        scratch = [pltpu.VMEM((blocks, rows, width), jnp.float32)] + scratch
    pairs = blocks * (levels + 1) * rows * queries
    return pl.pallas_call(
        functools.partial(attention_kernel, rows, first_query, queries, query_at, last, together),
        out_shape=out_shape,
        in_specs=[pl.BlockSpec(memory_space=pltpu.SMEM)] + [whole] * (len(inputs) - 1),
        out_specs=out_specs,
        scratch_shapes=scratch,
        cost_estimate=pl.CostEstimate(flops=pairs * HD * 2 * 6 * 4, transcendentals=2 * pairs, bytes_accessed=8 << 20),
        compiler_params=pltpu.CompilerParams(vmem_limit_bytes=56 * 1024 * 1024),
    )(*inputs)


def swap(x):
    return jnp.concatenate([x[:, HD:], x[:, :HD]], axis=1)


def interleave(first, second):
    lane = lax.broadcasted_iota(jnp.int32, first.shape, 1)
    return jnp.where(lane < HD, first, swap(second)), jnp.where(lane < HD, swap(first), second)


def pack_kernel(heads, pieces, *refs):
    inputs, out = refs[:-1], refs[-1]
    at = 0
    for first, second, low, count in pieces:
        for pair in range(heads // 2):
            lanes = slice(pair * 2 * HD, (pair + 1) * 2 * HD)
            both = interleave(inputs[first][low : low + count, lanes], inputs[second][low : low + count, lanes])
            out[2 * pair, at : at + count, :] = both[0]
            out[2 * pair + 1, at : at + count, :] = both[1]
        at += count


def pack(arrays, pieces):
    heads = arrays[0].shape[1] // HD
    total = sum(piece[3] for piece in pieces)
    whole = pl.BlockSpec(memory_space=pltpu.VMEM)
    return pl.pallas_call(
        functools.partial(pack_kernel, heads, pieces),
        out_shape=jax.ShapeDtypeStruct((heads, total, 2 * HD), CAST),
        in_specs=[whole] * len(arrays),
        out_specs=whole,
        cost_estimate=pl.CostEstimate(flops=0, transcendentals=0, bytes_accessed=8 * total * heads * HD),
    )(*arrays)


def unpack_kernel(heads, rows, early, late, mixed, query_grad, key_grad, value_grad):
    half = early.shape[1]
    for pair in range(heads // 2):
        lanes = slice(pair * 2 * HD, (pair + 1) * 2 * HD)
        query_grad[:half, lanes], mixed[:half, lanes] = interleave(early[2 * pair], early[2 * pair + 1])
        query_grad[half:, lanes], mixed[half:, lanes] = interleave(late[2 * pair, rows:], late[2 * pair + 1, rows:])
        key_grad[:, lanes], value_grad[:, lanes] = interleave(late[2 * pair, :rows], late[2 * pair + 1, :rows])


def unpack(early, late, rows):
    heads = early.shape[0]
    whole = pl.BlockSpec(memory_space=pltpu.VMEM)
    return pl.pallas_call(
        functools.partial(unpack_kernel, heads, rows),
        out_shape=(jax.ShapeDtypeStruct((rows, heads * HD), CAST),) * 4,
        in_specs=[whole] * 2,
        out_specs=(whole,) * 4,
    )(early, late)


def by_heads(packed):
    return lax.all_to_all(packed, "tm", split_axis=0, concat_axis=0, tiled=True)


def head_plan(queries, key_rows, value_rows, grad_output, extra_blocks):
    rows = queries.shape[0]
    half = rows // 2
    early = by_heads(
        pack((key_rows, value_rows, queries, grad_output), ((0, 1, 0, rows), (2, 3, 0, half)))
    )
    late_packed = pack((queries, grad_output), ((0, 1, half, half),))
    early, late_packed = lax.optimization_barrier((early, late_packed))
    late = by_heads(late_packed)
    early_rows, sums = attention(extra_blocks, early, early, None, rows, 0, half, rows, False)
    early_back = by_heads(early_rows)
    late_rows = attention(extra_blocks, early, late, sums, rows, half, half, 0, True)
    late_back = by_heads(late_rows)
    return unpack(early_back, late_back, rows)


def local(queries, key_rows, value_rows, grad_output, extra_blocks):
    if lax.axis_size("tm") == queries.shape[1] // HD:
        return head_plan(queries, key_rows, value_rows, grad_output, extra_blocks)
    return block_plan(queries, key_rows, value_rows, grad_output, extra_blocks)


def solution(mesh):
    placed = (
        P(("member", "tm"), None),
        P(("member", "tm"), None),
        P(("member", "tm"), None),
        P(("member", "tm"), None),
        P("member", None),
    )
    return jax.shard_map(
        local,
        mesh=mesh,
        in_specs=placed,
        out_specs=(
            P(("member", "tm"), None),
            P(("member", "tm"), None),
            P(("member", "tm"), None),
            P(("member", "tm"), None),
        ),
        check_vma=False,
    )
```

```python
import functools
import math

import jax
import jax.numpy as jnp
from jax import lax
from jax.experimental import pallas as pl
from jax.experimental.pallas import tpu as pltpu
from jax.sharding import PartitionSpec as P

HD = 64
HG = 2
SUB = 16
CAP = 2
TILE = 256
LOWEST = -1e30
CAST = jnp.bfloat16
TOGETHER = 2


very_negative = -1e30


def from_behind(value, axis, by):
    peers = lax.axis_size(axis)
    pairs = [(i, i + by) for i in range(peers) if 0 <= i + by < peers]
    return lax.ppermute(value, axis, pairs)


def split_heads(values):
    return values.reshape(values.shape[0], values.shape[1] // HD, HD)


def forward_group(query_part, key_part, value_part, key_mask, scaling):
    scores = (
        jnp.einsum(
            "qhd,khd->hqk",
            split_heads(query_part),
            split_heads(key_part),
            preferred_element_type=jnp.float32,
        )
        * scaling
    )
    scores = jnp.where(key_mask[None], scores, very_negative)
    weights = jax.nn.softmax(scores, axis=-1)
    weights_low = weights.astype(jnp.bfloat16)
    mixed_heads = jnp.einsum(
        "hqk,khd->qhd", weights_low, split_heads(value_part), preferred_element_type=jnp.float32
    )
    mixed_part = mixed_heads.reshape(query_part.shape).astype(jnp.bfloat16)
    return (weights, weights_low, mixed_part)


def backward_group(
    query_part, key_part, value_part, grad_part, mixed_part, weights, weights_low, scaling
):
    grad_heads = split_heads(grad_part)
    row_delta = jnp.sum(
        grad_heads.astype(jnp.float32) * split_heads(mixed_part).astype(jnp.float32), axis=-1
    )
    row_delta = jnp.transpose(row_delta)[:, :, None]
    weight_grads = jnp.einsum(
        "qhd,khd->hqk", grad_heads, split_heads(value_part), preferred_element_type=jnp.float32
    )
    score_grads = (weights * (weight_grads - row_delta)).astype(jnp.bfloat16)
    query_grads = (
        jnp.einsum(
            "hqk,khd->qhd", score_grads, split_heads(key_part), preferred_element_type=jnp.float32
        )
        * scaling
    )
    key_grads = (
        jnp.einsum(
            "hqk,qhd->khd", score_grads, split_heads(query_part), preferred_element_type=jnp.float32
        )
        * scaling
    )
    value_grads = jnp.einsum(
        "hqk,qhd->khd", weights_low, grad_heads, preferred_element_type=jnp.float32
    )
    return (
        query_grads.reshape(query_part.shape),
        key_grads.reshape(key_part.shape),
        value_grads.reshape(key_part.shape),
    )


def block_plan(queries, key_rows, value_rows, grad_output, extra_blocks):
    devices = lax.axis_size("tm")
    position = lax.axis_index("tm")
    block_rows = queries.shape[0]
    model_width = queries.shape[1]
    per_block = block_rows // SUB
    group_width = HG * HD
    group_count = model_width // group_width
    scaling = 1.0 / math.sqrt(HD)
    distances = []
    reach = 1
    while reach < devices:
        distances.append(reach)
        reach = reach * 2
    key_value = jnp.concatenate([key_rows, value_rows], axis=1)
    partner_blocks = [from_behind(key_value, "tm", distance) for distance in distances]
    owner_table = jnp.where(extra_blocks >= 0, extra_blocks // per_block, -1)
    inside_table = jnp.where(extra_blocks >= 0, extra_blocks % per_block, 0)
    owned_here = owner_table == position
    ranked = jnp.cumsum(owned_here.astype(jnp.int32), axis=1) - 1
    slot_ids = jnp.arange(CAP, dtype=jnp.int32)
    chosen = owned_here[:, None, :] & (ranked[:, None, :] == slot_ids[None, :, None])
    send_valid = jnp.any(chosen, axis=2)
    send_index = jnp.sum(jnp.where(chosen, inside_table[:, None, :], 0), axis=2)
    key_value_subs = key_value.reshape(per_block, SUB * 2 * model_width)
    send_rows = jnp.take(key_value_subs, send_index.reshape(-1), axis=0).reshape(
        devices * CAP * SUB, 2 * model_width
    )
    extra_rows = lax.all_to_all(send_rows, "tm", split_axis=0, concat_axis=0, tiled=True)
    my_owners = lax.dynamic_index_in_dim(owner_table, position, 0, keepdims=False)
    owner_ids = jnp.arange(devices, dtype=jnp.int32)
    taken_count = jnp.sum((my_owners[None, :] == owner_ids[:, None]).astype(jnp.int32), axis=1)
    slot_live = taken_count[:, None] > slot_ids[None, :]
    extra_live = jnp.repeat(slot_live.reshape(-1), SUB)
    row_ids = jnp.arange(block_rows, dtype=jnp.int32)
    own_mask = row_ids[:, None] >= row_ids[None, :]
    partner_live = jnp.concatenate(
        [jnp.broadcast_to(position >= distance, (block_rows,)) for distance in distances]
    )
    far_live = jnp.concatenate([partner_live, extra_live])
    key_mask = jnp.concatenate(
        [own_mask, jnp.broadcast_to(far_live[None, :], (block_rows, far_live.shape[0]))], axis=1
    )
    all_keys = jnp.concatenate([key_value] + partner_blocks + [extra_rows], axis=0)

    def columns(array, group_index, offset):
        return array[
            :, offset + group_index * group_width : offset + (group_index + 1) * group_width
        ]

    mixed_parts, query_parts, key_parts, value_parts = ([], [], [], [])
    for group_index in range(group_count):
        query_part = columns(queries, group_index, 0)
        key_part = columns(all_keys, group_index, 0)
        value_part = columns(all_keys, group_index, model_width)
        weights, weights_low, mixed_part = forward_group(
            query_part, key_part, value_part, key_mask, scaling
        )
        mixed_parts.append(mixed_part)
        grads = backward_group(
            query_part,
            key_part,
            value_part,
            columns(grad_output, group_index, 0),
            mixed_part,
            weights,
            weights_low,
            scaling,
        )
        query_parts.append(grads[0])
        key_parts.append(grads[1])
        value_parts.append(grads[2])
    mixed_rows = jnp.concatenate(mixed_parts, axis=1)
    query_grad = jnp.concatenate(query_parts, axis=1).astype(jnp.bfloat16)
    grads_all = jnp.concatenate(
        [jnp.concatenate(key_parts, axis=1), jnp.concatenate(value_parts, axis=1)], axis=1
    )
    grad_total = grads_all[:block_rows]
    partner_terms = [
        grads_all[(1 + level) * block_rows : (2 + level) * block_rows]
        for level in range(len(distances))
    ]
    extra_terms = grads_all[(1 + len(distances)) * block_rows :]
    for level, distance in enumerate(distances):
        returned = from_behind(partner_terms[level].astype(jnp.bfloat16), "tm", -distance)
        grad_total = grad_total + returned.astype(jnp.float32)
    extra_back = lax.all_to_all(
        extra_terms.astype(jnp.bfloat16), "tm", split_axis=0, concat_axis=0, tiled=True
    )
    sub_ids = jnp.arange(per_block, dtype=jnp.int32)
    one_hot = (
        (send_index.reshape(-1)[None, :] == sub_ids[:, None]) & send_valid.reshape(-1)[None, :]
    ).astype(jnp.bfloat16)
    folded = jnp.dot(
        one_hot,
        extra_back.reshape(devices * CAP, SUB * 2 * model_width),
        preferred_element_type=jnp.float32,
    )
    grad_total = grad_total + folded.reshape(block_rows, 2 * model_width)
    key_grad = grad_total[:, :model_width].astype(jnp.bfloat16)
    value_grad = grad_total[:, model_width:].astype(jnp.bfloat16)
    return (mixed_rows, query_grad, key_grad, value_grad)


def nn(a, b):
    return lax.dot_general(a, b, (((1,), (0,)), ((), ())), preferred_element_type=jnp.float32)


def by_eights(x, op):
    parts = [x[i : i + 8] for i in range(0, x.shape[0], 8)]
    while len(parts) > 1:
        parts = [op(*parts[i : i + 2]) if i + 1 < len(parts) else parts[i] for i in range(0, len(parts), 2)]
    return parts[0]


def wrapped(i, count):
    return jnp.where(i < 0, i + count, jnp.where(i >= count, i - count, i))


class Block:
    def __init__(self, b, partners, rows, first_query, table, kv, kv_t, block, scores, gathered, sg, wl, dacc):
        self.kv, self.kv_t, self.scores, self.gathered, self.dacc, self.b = kv, kv_t, scores, gathered, dacc, b
        self.sg, self.wl = sg, wl
        self.queries = queries = block.shape[0]
        width = 2 * HD
        scaling = 1.0 / math.sqrt(HD)
        lane = lax.broadcasted_iota(jnp.int32, block.shape, 1)
        zero = jnp.zeros_like(block)
        q_part = jnp.where(lane < HD, block * CAST(scaling), zero)
        g_part = jnp.where(lane < HD, zero, block)
        self.qg_part = jnp.concatenate([q_part, g_part], axis=0)
        self.block_t = jnp.transpose(block.astype(jnp.float32))
        row_t = lax.broadcasted_iota(jnp.int32, (width, queries), 0)
        self.q_t = jnp.where(row_t < HD, self.block_t * scaling, 0.0).astype(CAST)
        self.g_t = jnp.where(row_t < HD, 0.0, self.block_t).astype(CAST)
        self.chunks = []
        if first_query:
            self.chunks.append((b, 0, first_query, "all"))
        self.chunks.append((b, first_query, queries, "own"))
        for p in range(partners):
            self.chunks.append((b - (1 << p), 0, rows, "all"))
        self.extra_places = []
        entries = min(table.shape[1], CAP * ((1 << partners) - 1))
        if partners:
            self.live = jnp.int32(0)
            for e in range(entries):
                entry = table[b, e]
                self.live = self.live + (entry >= 0).astype(jnp.int32)
                entry = jnp.maximum(entry, 0)
                place = (entry // (rows // SUB), pl.multiple_of(entry % (rows // SUB) * SUB, SUB))
                self.extra_places.append(place)
                gathered[e * SUB : (e + 1) * SUB, :] = kv[place[0], pl.ds(place[1], SUB), :]
            self.gathered_t = jnp.transpose(gathered[: entries * SUB, :].astype(jnp.float32)).astype(CAST)
            self.chunks.append((None, 0, entries * SUB, "extra"))
        self.places = []
        at = 0
        for chunk in self.chunks:
            self.places.append(slice(at, at + chunk[2]))
            at += chunk[2]

    def keys(self, chunk):
        block, first, count, kind = chunk
        if kind == "extra":
            return self.gathered[:count, :]
        return self.kv[block, first : first + count, :]

    def keys_t(self, chunk):
        block, first, count, kind = chunk
        if kind == "extra":
            return self.gathered_t
        return self.kv_t[block, :, first : first + count]

    def score(self):
        peak = jnp.full((8, self.queries), LOWEST, jnp.float32)
        for chunk, place in zip(self.chunks, self.places):
            s = nn(self.keys(chunk), self.q_t)
            row = lax.broadcasted_iota(jnp.int32, s.shape, 0)
            if chunk[3] == "own":
                s = jnp.where(row <= lax.broadcasted_iota(jnp.int32, s.shape, 1), s, LOWEST)
            if chunk[3] == "extra":
                s = jnp.where(row < self.live * SUB, s, LOWEST)
            self.scores[place, :] = s
            peak = jnp.maximum(peak, by_eights(s, jnp.maximum))
        self.top = jnp.max(peak, axis=0, keepdims=True)

    def mix(self):
        total = jnp.zeros((8, self.queries), jnp.float32)
        mixed = jnp.zeros((HD, self.queries), jnp.float32)
        for chunk, place in zip(self.chunks, self.places):
            w = jnp.exp(self.scores[place, :] - self.top)
            total = total + by_eights(w, jnp.add)
            mixed = mixed + nn(self.keys_t(chunk)[HD:], w.astype(CAST))
        total = jnp.sum(total, axis=0, keepdims=True)
        self.mixed = mixed / total
        low = self.mixed.astype(CAST).astype(jnp.float32)
        self.delta = jnp.sum(self.block_t[HD:] * low, axis=0, keepdims=True)
        self.norm = self.top + jnp.log(total)

    def grads(self):
        query_grad = jnp.zeros((HD, self.queries), jnp.float32)
        for chunk, place in zip(self.chunks, self.places):
            w = jnp.exp(self.scores[place, :] - self.norm)
            self.sg[place, :] = (w * (nn(self.keys(chunk), self.g_t) - self.delta)).astype(CAST)
            self.wl[place, :] = w.astype(CAST)
        for chunk, place in zip(self.chunks, self.places):
            sg = self.sg[place, :]
            query_grad = query_grad + nn(self.keys_t(chunk)[:HD], sg)
            part = nn(jnp.concatenate([sg, self.wl[place, :]], axis=1), self.qg_part)
            block, first, count, kind = chunk
            if kind == "extra":
                for e, (owner, at) in enumerate(self.extra_places):
                    self.dacc[owner, pl.ds(at, SUB), :] += part[e * SUB : (e + 1) * SUB]
            else:
                self.dacc[block, first : first + count, :] += part
        return jnp.transpose(jnp.concatenate([query_grad * (1.0 / math.sqrt(HD)), self.mixed], axis=0)).astype(CAST)


def attention_kernel(blocks, rows, first_query, queries, together, *refs):
    last = first_query + queries == rows
    refs = list(refs)

    def take(n):
        got = refs[:n]
        del refs[:n]
        return got

    me_ref, table = take(2)
    early = take(blocks)
    me = me_ref[0]
    if last:
        qd, before = take(2)
        out = take(blocks)
        kv, kv_t, scores, gathered, sg, wl, dacc, oq = take(8)
        dacc[...] = before[...]
    else:
        oq, dacc, kv, kv_t, scores, gathered, sg, wl, qd = take(9)
        dacc[...] = jnp.zeros_like(dacc)
    for k in range(blocks):
        b = wrapped(me - k, blocks)
        keys = early[k][:rows, :]
        kv[b] = keys
        kv_t[b] = jnp.transpose(keys.astype(jnp.float32)).astype(CAST)
        if not last:
            qd[b] = early[k][rows:, :]
    levels = (blocks - 1).bit_length()

    def run(partners, ids):
        work = [
            Block(b, partners, rows, first_query, table, kv, kv_t, qd[b], scores.at[i], gathered.at[i], sg.at[i],
                  wl.at[i], dacc)
            for i, b in enumerate(ids)
        ]
        for w in work:
            w.score()
        for w in work:
            w.mix()
        for w in work:
            oq[w.b] = w.grads()

    for partners in range(levels, -1, -1):
        low = (1 << partners) >> 1
        high = min(1 << partners, blocks)
        group = math.gcd(together, high - low)

        def step(i, carry, partners=partners, high=high, group=group):
            run(partners, [high - 1 - i * group - j for j in range(group)])
            return carry

        if high - low > group:
            lax.fori_loop(0, (high - low) // group, step, 0)
        else:
            run(partners, [jnp.int32(high - 1 - j) for j in range(group)])
    if last:
        for k in range(blocks):
            b = wrapped(me + k, blocks)
            out[k][:rows, :] = dacc[b].astype(CAST)
            out[k][rows:, :] = oq[b]


def attention(me, table, early, late, before, rows, first_query, queries, together=None):
    together = TOGETHER if together is None else together
    blocks = len(early)
    width = early[0].shape[1]
    entries = table.shape[1]
    levels = (blocks - 1).bit_length()
    last = first_query + queries == rows
    whole = pl.BlockSpec(memory_space=pltpu.VMEM)
    small = pl.BlockSpec(memory_space=pltpu.SMEM)
    sums = (blocks, rows, width)
    if last:
        out_shape = [jax.ShapeDtypeStruct((rows + queries, width), CAST)] * blocks
        inputs = [me, table] + list(early) + [late, before]
    else:
        out_shape = [jax.ShapeDtypeStruct((blocks, queries, width), CAST), jax.ShapeDtypeStruct(sums, jnp.float32)]
        inputs = [me, table] + list(early)
    extra_rows = min(entries, CAP * ((1 << levels) - 1)) * SUB
    list_rows = first_query + queries + levels * rows + extra_rows
    scratch = [
        pltpu.VMEM((blocks, rows, width), CAST),
        pltpu.VMEM((blocks, width, rows), CAST),
        pltpu.VMEM((together, list_rows, queries), jnp.float32),
        pltpu.VMEM((together, extra_rows, width), CAST),
        pltpu.VMEM((together, list_rows, queries), CAST),
        pltpu.VMEM((together, list_rows, queries), CAST),
    ]
    if last:
        scratch.append(pltpu.VMEM(sums, jnp.float32))
    scratch.append(pltpu.VMEM((blocks, queries, width), CAST))
    pairs = blocks * (levels + 1) * rows * queries
    return pl.pallas_call(
        functools.partial(attention_kernel, blocks, rows, first_query, queries, together),
        out_shape=tuple(out_shape),
        in_specs=[small] * 2 + [whole] * (len(inputs) - 2),
        out_specs=(whole,) * len(out_shape),
        scratch_shapes=scratch,
        cost_estimate=pl.CostEstimate(flops=pairs * HD * 2 * 6 * 4, transcendentals=2 * pairs, bytes_accessed=8 << 20),
        compiler_params=pltpu.CompilerParams(vmem_limit_bytes=56 * 1024 * 1024),
    )(*inputs)


def swap(x):
    return jnp.concatenate([x[:, HD:], x[:, :HD]], axis=1)


def interleave(first, second):
    lane = lax.broadcasted_iota(jnp.int32, first.shape, 1)
    return jnp.where(lane < HD, first, swap(second)), jnp.where(lane < HD, swap(first), second)


def pack_kernel(heads, pieces, apart, *refs):
    me = refs[0][0]
    inputs = refs[1 : 1 + 1 + max(max(piece[:2]) for piece in pieces)]
    packed = refs[-1]
    for pair in range(heads // 2):
        lanes = slice(pair * 2 * HD, (pair + 1) * 2 * HD)
        at = 0
        for first, second, low, count in pieces:
            both = interleave(inputs[first][low : low + count, lanes], inputs[second][low : low + count, lanes])
            packed[2 * pair, at : at + count, :] = both[0]
            packed[2 * pair + 1, at : at + count, :] = both[1]
            at += count
    if apart:
        for k, out in enumerate(refs[1 + len(inputs) : -1]):
            out[...] = packed[wrapped(me + k, heads)]


def pack(me, arrays, pieces, apart):
    heads = arrays[0].shape[1] // HD
    total = sum(piece[3] for piece in pieces)
    whole = pl.BlockSpec(memory_space=pltpu.VMEM)
    all_heads = (heads, total, 2 * HD)
    if apart:
        out_shape = (jax.ShapeDtypeStruct((total, 2 * HD), CAST),) * heads
        out_specs = (whole,) * heads
        scratch = [pltpu.VMEM(all_heads, CAST)]
    else:
        out_shape, out_specs, scratch = jax.ShapeDtypeStruct(all_heads, CAST), whole, []
    return pl.pallas_call(
        functools.partial(pack_kernel, heads, pieces, apart),
        out_shape=out_shape,
        in_specs=[pl.BlockSpec(memory_space=pltpu.SMEM)] + [whole] * len(arrays),
        out_specs=out_specs,
        scratch_shapes=scratch,
        cost_estimate=pl.CostEstimate(flops=0, transcendentals=0, bytes_accessed=8 * total * heads * HD),
    )(me, *arrays)


def unpack_kernel(heads, rows, *refs):
    me = refs[0][0]
    early, late = refs[1], refs[2 : 2 + heads]
    mixed, query_grad, key_grad, value_grad, ordered = refs[2 + heads :]
    for k in range(heads):
        ordered[wrapped(me - k, heads)] = late[k][...]
    half = early.shape[1]
    for pair in range(heads // 2):
        lanes = slice(pair * 2 * HD, (pair + 1) * 2 * HD)
        even, odd = ordered[2 * pair], ordered[2 * pair + 1]
        query_grad[:half, lanes], mixed[:half, lanes] = interleave(early[2 * pair], early[2 * pair + 1])
        query_grad[half:, lanes], mixed[half:, lanes] = interleave(even[rows:], odd[rows:])
        key_grad[:, lanes], value_grad[:, lanes] = interleave(even[:rows], odd[:rows])


def unpack(me, early, late, rows):
    heads = len(late)
    whole = pl.BlockSpec(memory_space=pltpu.VMEM)
    return pl.pallas_call(
        functools.partial(unpack_kernel, heads, rows),
        out_shape=(jax.ShapeDtypeStruct((rows, heads * HD), CAST),) * 4,
        in_specs=[pl.BlockSpec(memory_space=pltpu.SMEM)] + [whole] * (1 + heads),
        out_specs=(whole,) * 4,
        scratch_shapes=[pltpu.VMEM((heads,) + late[0].shape, CAST)],
    )(me, early, *late)


def shifted_all(pieces):
    count = len(pieces)
    return [pieces[0]] + [
        lax.ppermute(pieces[k], "tm", [(i, (i + k) % count) for i in range(count)]) for k in range(1, count)
    ]


def all_heads(packed):
    return lax.all_to_all(packed, "tm", split_axis=0, concat_axis=0, tiled=True)


def head_plan(queries, key_rows, value_rows, grad_output, extra_blocks):
    rows = queries.shape[0]
    half = rows // 2
    me = lax.axis_index("tm").astype(jnp.int32).reshape(1)
    early = shifted_all(
        pack(me, (key_rows, value_rows, queries, grad_output), ((0, 1, 0, rows), (2, 3, 0, half)), True)
    )
    late_packed = pack(me, (queries, grad_output), ((0, 1, half, half),), False)
    *early, late_packed = lax.optimization_barrier((*early, late_packed))
    late = all_heads(late_packed)
    early_rows, sums = attention(me, extra_blocks, early, None, None, rows, 0, half)
    early_back = all_heads(early_rows)
    late_rows = attention(me, extra_blocks, early, late, sums, rows, half, half)
    late_back = shifted_all(late_rows)
    return unpack(me, early_back, late_back, rows)


def local(queries, key_rows, value_rows, grad_output, extra_blocks):
    if lax.axis_size("tm") == queries.shape[1] // HD:
        return head_plan(queries, key_rows, value_rows, grad_output, extra_blocks)
    return block_plan(queries, key_rows, value_rows, grad_output, extra_blocks)


def solution(mesh):
    placed = (
        P(("member", "tm"), None),
        P(("member", "tm"), None),
        P(("member", "tm"), None),
        P(("member", "tm"), None),
        P("member", None),
    )
    return jax.shard_map(
        local,
        mesh=mesh,
        in_specs=placed,
        out_specs=(
            P(("member", "tm"), None),
            P(("member", "tm"), None),
            P(("member", "tm"), None),
            P(("member", "tm"), None),
        ),
        check_vma=False,
    )
```

```python
import functools
import math

import jax
import jax.numpy as jnp
from jax import lax
from jax.experimental import pallas as pl
from jax.experimental.pallas import tpu as pltpu
from jax.sharding import PartitionSpec as P

HD = 64
HG = 2
SUB = 16
CAP = 2
TILE = 256
LOWEST = -1e30
CAST = jnp.bfloat16
TOGETHER = 2


very_negative = -1e30


def from_behind(value, axis, by):
    peers = lax.axis_size(axis)
    pairs = [(i, i + by) for i in range(peers) if 0 <= i + by < peers]
    return lax.ppermute(value, axis, pairs)


def split_heads(values):
    return values.reshape(values.shape[0], values.shape[1] // HD, HD)


def forward_group(query_part, key_part, value_part, key_mask, scaling):
    scores = (
        jnp.einsum(
            "qhd,khd->hqk",
            split_heads(query_part),
            split_heads(key_part),
            preferred_element_type=jnp.float32,
        )
        * scaling
    )
    scores = jnp.where(key_mask[None], scores, very_negative)
    weights = jax.nn.softmax(scores, axis=-1)
    weights_low = weights.astype(jnp.bfloat16)
    mixed_heads = jnp.einsum(
        "hqk,khd->qhd", weights_low, split_heads(value_part), preferred_element_type=jnp.float32
    )
    mixed_part = mixed_heads.reshape(query_part.shape).astype(jnp.bfloat16)
    return (weights, weights_low, mixed_part)


def backward_group(
    query_part, key_part, value_part, grad_part, mixed_part, weights, weights_low, scaling
):
    grad_heads = split_heads(grad_part)
    row_delta = jnp.sum(
        grad_heads.astype(jnp.float32) * split_heads(mixed_part).astype(jnp.float32), axis=-1
    )
    row_delta = jnp.transpose(row_delta)[:, :, None]
    weight_grads = jnp.einsum(
        "qhd,khd->hqk", grad_heads, split_heads(value_part), preferred_element_type=jnp.float32
    )
    score_grads = (weights * (weight_grads - row_delta)).astype(jnp.bfloat16)
    query_grads = (
        jnp.einsum(
            "hqk,khd->qhd", score_grads, split_heads(key_part), preferred_element_type=jnp.float32
        )
        * scaling
    )
    key_grads = (
        jnp.einsum(
            "hqk,qhd->khd", score_grads, split_heads(query_part), preferred_element_type=jnp.float32
        )
        * scaling
    )
    value_grads = jnp.einsum(
        "hqk,qhd->khd", weights_low, grad_heads, preferred_element_type=jnp.float32
    )
    return (
        query_grads.reshape(query_part.shape),
        key_grads.reshape(key_part.shape),
        value_grads.reshape(key_part.shape),
    )


def block_plan(queries, key_rows, value_rows, grad_output, extra_blocks):
    devices = lax.axis_size("tm")
    position = lax.axis_index("tm")
    block_rows = queries.shape[0]
    model_width = queries.shape[1]
    per_block = block_rows // SUB
    group_width = HG * HD
    group_count = model_width // group_width
    scaling = 1.0 / math.sqrt(HD)
    distances = []
    reach = 1
    while reach < devices:
        distances.append(reach)
        reach = reach * 2
    key_value = jnp.concatenate([key_rows, value_rows], axis=1)
    partner_blocks = [from_behind(key_value, "tm", distance) for distance in distances]
    owner_table = jnp.where(extra_blocks >= 0, extra_blocks // per_block, -1)
    inside_table = jnp.where(extra_blocks >= 0, extra_blocks % per_block, 0)
    owned_here = owner_table == position
    ranked = jnp.cumsum(owned_here.astype(jnp.int32), axis=1) - 1
    slot_ids = jnp.arange(CAP, dtype=jnp.int32)
    chosen = owned_here[:, None, :] & (ranked[:, None, :] == slot_ids[None, :, None])
    send_valid = jnp.any(chosen, axis=2)
    send_index = jnp.sum(jnp.where(chosen, inside_table[:, None, :], 0), axis=2)
    key_value_subs = key_value.reshape(per_block, SUB * 2 * model_width)
    send_rows = jnp.take(key_value_subs, send_index.reshape(-1), axis=0).reshape(
        devices * CAP * SUB, 2 * model_width
    )
    extra_rows = lax.all_to_all(send_rows, "tm", split_axis=0, concat_axis=0, tiled=True)
    my_owners = lax.dynamic_index_in_dim(owner_table, position, 0, keepdims=False)
    owner_ids = jnp.arange(devices, dtype=jnp.int32)
    taken_count = jnp.sum((my_owners[None, :] == owner_ids[:, None]).astype(jnp.int32), axis=1)
    slot_live = taken_count[:, None] > slot_ids[None, :]
    extra_live = jnp.repeat(slot_live.reshape(-1), SUB)
    row_ids = jnp.arange(block_rows, dtype=jnp.int32)
    own_mask = row_ids[:, None] >= row_ids[None, :]
    partner_live = jnp.concatenate(
        [jnp.broadcast_to(position >= distance, (block_rows,)) for distance in distances]
    )
    far_live = jnp.concatenate([partner_live, extra_live])
    key_mask = jnp.concatenate(
        [own_mask, jnp.broadcast_to(far_live[None, :], (block_rows, far_live.shape[0]))], axis=1
    )
    all_keys = jnp.concatenate([key_value] + partner_blocks + [extra_rows], axis=0)

    def columns(array, group_index, offset):
        return array[
            :, offset + group_index * group_width : offset + (group_index + 1) * group_width
        ]

    mixed_parts, query_parts, key_parts, value_parts = ([], [], [], [])
    for group_index in range(group_count):
        query_part = columns(queries, group_index, 0)
        key_part = columns(all_keys, group_index, 0)
        value_part = columns(all_keys, group_index, model_width)
        weights, weights_low, mixed_part = forward_group(
            query_part, key_part, value_part, key_mask, scaling
        )
        mixed_parts.append(mixed_part)
        grads = backward_group(
            query_part,
            key_part,
            value_part,
            columns(grad_output, group_index, 0),
            mixed_part,
            weights,
            weights_low,
            scaling,
        )
        query_parts.append(grads[0])
        key_parts.append(grads[1])
        value_parts.append(grads[2])
    mixed_rows = jnp.concatenate(mixed_parts, axis=1)
    query_grad = jnp.concatenate(query_parts, axis=1).astype(jnp.bfloat16)
    grads_all = jnp.concatenate(
        [jnp.concatenate(key_parts, axis=1), jnp.concatenate(value_parts, axis=1)], axis=1
    )
    grad_total = grads_all[:block_rows]
    partner_terms = [
        grads_all[(1 + level) * block_rows : (2 + level) * block_rows]
        for level in range(len(distances))
    ]
    extra_terms = grads_all[(1 + len(distances)) * block_rows :]
    for level, distance in enumerate(distances):
        returned = from_behind(partner_terms[level].astype(jnp.bfloat16), "tm", -distance)
        grad_total = grad_total + returned.astype(jnp.float32)
    extra_back = lax.all_to_all(
        extra_terms.astype(jnp.bfloat16), "tm", split_axis=0, concat_axis=0, tiled=True
    )
    sub_ids = jnp.arange(per_block, dtype=jnp.int32)
    one_hot = (
        (send_index.reshape(-1)[None, :] == sub_ids[:, None]) & send_valid.reshape(-1)[None, :]
    ).astype(jnp.bfloat16)
    folded = jnp.dot(
        one_hot,
        extra_back.reshape(devices * CAP, SUB * 2 * model_width),
        preferred_element_type=jnp.float32,
    )
    grad_total = grad_total + folded.reshape(block_rows, 2 * model_width)
    key_grad = grad_total[:, :model_width].astype(jnp.bfloat16)
    value_grad = grad_total[:, model_width:].astype(jnp.bfloat16)
    return (mixed_rows, query_grad, key_grad, value_grad)


def nn(a, b):
    return lax.dot_general(a, b, (((1,), (0,)), ((), ())), preferred_element_type=jnp.float32)


def by_eights(x, op):
    parts = [x[i : i + 8] for i in range(0, x.shape[0], 8)]
    while len(parts) > 1:
        parts = [op(*parts[i : i + 2]) if i + 1 < len(parts) else parts[i] for i in range(0, len(parts), 2)]
    return parts[0]


def wrapped(i, count):
    return jnp.where(i < 0, i + count, jnp.where(i >= count, i - count, i))


def in_turn(*steps):
    steps = list(steps)
    while steps:
        for step in list(steps):
            if next(step, steps) is steps:
                steps.remove(step)


class Block:
    def __init__(self, b, partners, rows, first_query, table, kv, kv_t, block, scores, gathered, sg, wl, dacc, oq):
        self.oq = oq
        self.kv, self.kv_t, self.scores, self.gathered, self.dacc, self.b = kv, kv_t, scores, gathered, dacc, b
        self.sg, self.wl = sg, wl
        self.queries = queries = block.shape[0]
        width = 2 * HD
        scaling = 1.0 / math.sqrt(HD)
        lane = lax.broadcasted_iota(jnp.int32, block.shape, 1)
        zero = jnp.zeros_like(block)
        q_part = jnp.where(lane < HD, block * CAST(scaling), zero)
        g_part = jnp.where(lane < HD, zero, block)
        self.qg_part = jnp.concatenate([q_part, g_part], axis=0)
        self.block_t = jnp.transpose(block.astype(jnp.float32))
        row_t = lax.broadcasted_iota(jnp.int32, (width, queries), 0)
        self.q_t = jnp.where(row_t < HD, self.block_t * scaling, 0.0).astype(CAST)
        self.g_t = jnp.where(row_t < HD, 0.0, self.block_t).astype(CAST)
        self.chunks = []
        if first_query:
            self.chunks.append((b, 0, first_query, "all"))
        self.chunks.append((b, first_query, queries, "own"))
        for p in range(partners):
            self.chunks.append((b - (1 << p), 0, rows, "all"))
        self.extra_places = []
        entries = min(table.shape[1], CAP * ((1 << partners) - 1))
        if partners:
            self.live = jnp.int32(0)
            for e in range(entries):
                entry = table[b, e]
                self.live = self.live + (entry >= 0).astype(jnp.int32)
                entry = jnp.maximum(entry, 0)
                place = (entry // (rows // SUB), pl.multiple_of(entry % (rows // SUB) * SUB, SUB))
                self.extra_places.append(place)
                gathered[e * SUB : (e + 1) * SUB, :] = kv[place[0], pl.ds(place[1], SUB), :]
            self.gathered_t = jnp.transpose(gathered[: entries * SUB, :])
            self.chunks.append((None, 0, entries * SUB, "extra"))
        self.places = []
        at = 0
        for chunk in self.chunks:
            self.places.append(slice(at, at + chunk[2]))
            at += chunk[2]

    def keys(self, chunk):
        block, first, count, kind = chunk
        if kind == "extra":
            return self.gathered[:count, :]
        return self.kv[block, first : first + count, :]

    def keys_t(self, chunk):
        block, first, count, kind = chunk
        if kind == "extra":
            return self.gathered_t
        return self.kv_t[block, :, first : first + count]

    def score(self):
        peak = jnp.full((8, self.queries), LOWEST, jnp.float32)
        for chunk, place in zip(self.chunks, self.places):
            s = nn(self.keys(chunk), self.q_t)
            row = lax.broadcasted_iota(jnp.int32, s.shape, 0)
            if chunk[3] == "own":
                s = jnp.where(row <= lax.broadcasted_iota(jnp.int32, s.shape, 1), s, LOWEST)
            if chunk[3] == "extra":
                s = jnp.where(row < self.live * SUB, s, LOWEST)
            self.scores[place, :] = s
            peak = jnp.maximum(peak, by_eights(s, jnp.maximum))
            yield
        self.top = jnp.max(peak, axis=0, keepdims=True)

    def mix(self):
        total = jnp.zeros((8, self.queries), jnp.float32)
        mixed = jnp.zeros((HD, self.queries), jnp.float32)
        for chunk, place in zip(self.chunks, self.places):
            w = jnp.exp(self.scores[place, :] - self.top)
            total = total + by_eights(w, jnp.add)
            mixed = mixed + nn(self.keys_t(chunk)[HD:], w.astype(CAST))
            yield
        total = jnp.sum(total, axis=0, keepdims=True)
        self.mixed = mixed / total
        low = self.mixed.astype(CAST).astype(jnp.float32)
        self.delta = jnp.sum(self.block_t[HD:] * low, axis=0, keepdims=True)
        self.norm = self.top + jnp.log(total)

    def factors(self):
        for chunk, place in zip(self.chunks, self.places):
            w = jnp.exp(self.scores[place, :] - self.norm)
            self.sg[place, :] = (w * (nn(self.keys(chunk), self.g_t) - self.delta)).astype(CAST)
            self.wl[place, :] = w.astype(CAST)
            yield

    def products(self):
        query_grad = jnp.zeros((HD, self.queries), jnp.float32)
        for chunk, place in zip(self.chunks, self.places):
            sg = self.sg[place, :]
            query_grad = query_grad + nn(self.keys_t(chunk)[:HD], sg)
            part = nn(jnp.concatenate([sg, self.wl[place, :]], axis=1), self.qg_part)
            block, first, count, kind = chunk
            if kind == "extra":
                for e, (owner, at) in enumerate(self.extra_places):
                    self.dacc[owner, pl.ds(at, SUB), :] += part[e * SUB : (e + 1) * SUB]
            else:
                self.dacc[block, first : first + count, :] += part
            yield
        both = jnp.concatenate([query_grad * (1.0 / math.sqrt(HD)), self.mixed], axis=0)
        self.oq[self.b] = jnp.transpose(both).astype(CAST)


def attention_kernel(blocks, rows, first_query, queries, together, *refs):
    last = first_query + queries == rows
    refs = list(refs)

    def take(n):
        got = refs[:n]
        del refs[:n]
        return got

    me_ref, table = take(2)
    early = take(blocks)
    me = me_ref[0]
    if last:
        qd, sums = take(2)
        out = take(blocks)
        kv, kv_t, scores, gathered, sg, wl, dacc, held, moved, oq = take(10)
        for b in range(blocks):
            pltpu.make_async_copy(sums.at[b], held.at[b], moved.at[b]).start()
    else:
        oq, sums, kv, kv_t, scores, gathered, sg, wl, dacc, held, moved, qd = take(12)
    dacc[...] = jnp.zeros_like(dacc)
    for k in range(blocks):
        b = wrapped(me - k, blocks)
        keys = early[k][:rows, :]
        kv[b] = keys
        kv_t[b] = jnp.transpose(keys)
        if not last:
            qd[b] = early[k][rows:, :]
    levels = (blocks - 1).bit_length()

    def run(partners, ids):
        work = [
            Block(b, partners, rows, first_query, table, kv, kv_t, qd[b], scores.at[i], gathered.at[i], sg.at[i],
                  wl.at[i], dacc, oq)
            for i, b in enumerate(ids)
        ]
        for w in work:
            in_turn(w.score())
        for w in work:
            in_turn(w.mix())
        in_turn(work[0].factors())
        for now, then in zip(work, work[1:] + [None]):
            if then:
                in_turn(then.factors(), now.products())
            else:
                in_turn(now.products())
        if not last:
            for w in work:
                held[w.b] = dacc[w.b]
                pltpu.make_async_copy(held.at[w.b], sums.at[w.b], moved.at[w.b]).start()

    for partners in range(levels, -1, -1):
        low = (1 << partners) >> 1
        high = min(1 << partners, blocks)
        group = math.gcd(together, high - low)

        def step(i, carry, partners=partners, high=high, group=group):
            run(partners, [high - 1 - i * group - j for j in range(group)])
            return carry

        if high - low > group:
            lax.fori_loop(0, (high - low) // group, step, 0)
        else:
            run(partners, [jnp.int32(high - 1 - j) for j in range(group)])
    for b in range(blocks):
        if last:
            pltpu.make_async_copy(sums.at[b], held.at[b], moved.at[b]).wait()
        else:
            pltpu.make_async_copy(held.at[b], sums.at[b], moved.at[b]).wait()
    if last:
        for k in range(blocks):
            b = wrapped(me + k, blocks)
            out[k][:rows, :] = (dacc[b] + held[b]).astype(CAST)
            out[k][rows:, :] = oq[b]


def attention(me, table, early, late, before, rows, first_query, queries, together=None):
    together = TOGETHER if together is None else together
    blocks = len(early)
    width = early[0].shape[1]
    entries = table.shape[1]
    levels = (blocks - 1).bit_length()
    last = first_query + queries == rows
    whole = pl.BlockSpec(memory_space=pltpu.VMEM)
    small = pl.BlockSpec(memory_space=pltpu.SMEM)
    apart = pl.BlockSpec(memory_space=pl.ANY)
    sums = (blocks, rows, width)
    if last:
        out_shape = [jax.ShapeDtypeStruct((rows + queries, width), CAST)] * blocks
        inputs = [me, table] + list(early) + [late, before]
    else:
        out_shape = [jax.ShapeDtypeStruct((blocks, queries, width), CAST), jax.ShapeDtypeStruct(sums, jnp.float32)]
        inputs = [me, table] + list(early)
    extra_rows = min(entries, CAP * ((1 << levels) - 1)) * SUB
    list_rows = first_query + queries + levels * rows + extra_rows
    scratch = [
        pltpu.VMEM((blocks, rows, width), CAST),
        pltpu.VMEM((blocks, width, rows), CAST),
        pltpu.VMEM((together, list_rows, queries), jnp.float32),
        pltpu.VMEM((together, extra_rows, width), CAST),
        pltpu.VMEM((together, list_rows, queries), CAST),
        pltpu.VMEM((together, list_rows, queries), CAST),
    ]
    scratch += [pltpu.VMEM(sums, jnp.float32)] * 2 + [pltpu.SemaphoreType.DMA((blocks,))]
    scratch.append(pltpu.VMEM((blocks, queries, width), CAST))
    pairs = blocks * (levels + 1) * rows * queries
    return pl.pallas_call(
        functools.partial(attention_kernel, blocks, rows, first_query, queries, together),
        out_shape=tuple(out_shape),
        in_specs=[small] * 2 + [whole] * (len(inputs) - 3) + [apart if last else whole],
        out_specs=(whole,) * (len(out_shape) - 1) + (whole if last else apart,),
        scratch_shapes=scratch,
        cost_estimate=pl.CostEstimate(flops=pairs * HD * 2 * 6 * 4, transcendentals=2 * pairs, bytes_accessed=8 << 20),
        compiler_params=pltpu.CompilerParams(vmem_limit_bytes=56 * 1024 * 1024),
    )(*inputs)


def swap(x):
    return jnp.concatenate([x[:, HD:], x[:, :HD]], axis=1)


def interleave(first, second):
    lane = lax.broadcasted_iota(jnp.int32, first.shape, 1)
    return jnp.where(lane < HD, first, swap(second)), jnp.where(lane < HD, swap(first), second)


def pack_kernel(heads, pieces, apart, count, *refs):
    me = refs[0][0]
    sources, results = refs[1 : 1 + count], refs[1 + count : -3]
    packed, inputs, arrived = refs[-3:]
    rows = sources[0].shape[0]
    parts = 2

    def copy(i, part):
        place = pl.ds(part * (rows // parts), rows // parts)
        return pltpu.make_async_copy(sources[i].at[place], inputs.at[i, place], arrived.at[i * parts + part])

    for i in range(count):
        for part in range(parts):
            copy(i, part).start()
    ready = set()
    at = 0
    for first, second, low, size in pieces:
        for i in (first, second):
            if i not in ready:
                for part in range(parts):
                    copy(i, part).wait()
                ready.add(i)
        for pair in range(heads // 2):
            lanes = slice(pair * 2 * HD, (pair + 1) * 2 * HD)
            both = interleave(inputs[first, low : low + size, lanes], inputs[second, low : low + size, lanes])
            packed[2 * pair, at : at + size, :] = both[0]
            packed[2 * pair + 1, at : at + size, :] = both[1]
        at += size
    if apart:
        for k, out in enumerate(results):
            out[...] = packed[wrapped(me + k, heads)]
    else:
        results[0][...] = packed[...]


def pack(me, arrays, pieces, apart):
    rows, columns = arrays[0].shape
    heads = columns // HD
    total = sum(piece[3] for piece in pieces)
    whole = pl.BlockSpec(memory_space=pltpu.VMEM)
    all_heads = (heads, total, 2 * HD)
    if apart:
        out_shape = (jax.ShapeDtypeStruct((total, 2 * HD), CAST),) * heads
        out_specs = (whole,) * heads
    else:
        out_shape, out_specs = jax.ShapeDtypeStruct(all_heads, CAST), whole
    return pl.pallas_call(
        functools.partial(pack_kernel, heads, pieces, apart, len(arrays)),
        out_shape=out_shape,
        in_specs=[pl.BlockSpec(memory_space=pltpu.SMEM)] + [pl.BlockSpec(memory_space=pl.ANY)] * len(arrays),
        out_specs=out_specs,
        scratch_shapes=[
            pltpu.VMEM(all_heads, CAST),
            pltpu.VMEM((len(arrays), rows, columns), CAST),
            pltpu.SemaphoreType.DMA((2 * len(arrays),)),
        ],
        compiler_params=pltpu.CompilerParams(vmem_limit_bytes=56 * 1024 * 1024),
        cost_estimate=pl.CostEstimate(flops=0, transcendentals=0, bytes_accessed=8 * total * heads * HD),
    )(me, *arrays)


def unpack_kernel(heads, rows, *refs):
    me = refs[0][0]
    early, late = refs[1], refs[2 : 2 + heads]
    mixed, query_grad, key_grad, value_grad, ordered = refs[2 + heads :]
    for k in range(heads):
        ordered[wrapped(me - k, heads)] = late[k][...]
    half = early.shape[1]
    for pair in range(heads // 2):
        lanes = slice(pair * 2 * HD, (pair + 1) * 2 * HD)
        even, odd = ordered[2 * pair], ordered[2 * pair + 1]
        query_grad[:half, lanes], mixed[:half, lanes] = interleave(early[2 * pair], early[2 * pair + 1])
        query_grad[half:, lanes], mixed[half:, lanes] = interleave(even[rows:], odd[rows:])
        key_grad[:, lanes], value_grad[:, lanes] = interleave(even[:rows], odd[:rows])


def unpack(me, early, late, rows):
    heads = len(late)
    whole = pl.BlockSpec(memory_space=pltpu.VMEM)
    return pl.pallas_call(
        functools.partial(unpack_kernel, heads, rows),
        out_shape=(jax.ShapeDtypeStruct((rows, heads * HD), CAST),) * 4,
        in_specs=[pl.BlockSpec(memory_space=pltpu.SMEM)] + [whole] * (1 + heads),
        out_specs=(whole,) * 4,
        scratch_shapes=[pltpu.VMEM((heads,) + late[0].shape, CAST)],
        compiler_params=pltpu.CompilerParams(vmem_limit_bytes=10 * 1024 * 1024),
    )(me, early, *late)


def shifted_all(pieces):
    count = len(pieces)
    return [pieces[0]] + [
        lax.ppermute(pieces[k], "tm", [(i, (i + k) % count) for i in range(count)]) for k in range(1, count)
    ]


def all_heads(packed):
    return lax.all_to_all(packed, "tm", split_axis=0, concat_axis=0, tiled=True)


def head_plan(queries, key_rows, value_rows, grad_output, extra_blocks):
    rows = queries.shape[0]
    half = rows // 2
    me = lax.axis_index("tm").astype(jnp.int32).reshape(1)
    early = shifted_all(
        pack(me, (key_rows, value_rows, queries, grad_output), ((0, 1, 0, rows), (2, 3, 0, half)), True)
    )
    late_packed = pack(me, (queries, grad_output), ((0, 1, half, half),), False)
    *early, late_packed = lax.optimization_barrier((*early, late_packed))
    late = all_heads(late_packed)
    early_rows, sums = attention(me, extra_blocks, early, None, None, rows, 0, half)
    early_back = all_heads(early_rows)
    late_rows = attention(me, extra_blocks, early, late, sums, rows, half, half)
    late_back = shifted_all(late_rows)
    return unpack(me, early_back, late_back, rows)


def local(queries, key_rows, value_rows, grad_output, extra_blocks):
    if lax.axis_size("tm") == queries.shape[1] // HD:
        return head_plan(queries, key_rows, value_rows, grad_output, extra_blocks)
    return block_plan(queries, key_rows, value_rows, grad_output, extra_blocks)


def solution(mesh):
    placed = (
        P(("member", "tm"), None),
        P(("member", "tm"), None),
        P(("member", "tm"), None),
        P(("member", "tm"), None),
        P("member", None),
    )
    return jax.shard_map(
        local,
        mesh=mesh,
        in_specs=placed,
        out_specs=(
            P(("member", "tm"), None),
            P(("member", "tm"), None),
            P(("member", "tm"), None),
            P(("member", "tm"), None),
        ),
        check_vma=False,
    )
```

```python
import functools
import math

import jax
import jax.numpy as jnp
from jax import lax
from jax.experimental import pallas as pl
from jax.experimental.pallas import tpu as pltpu
from jax.sharding import PartitionSpec as P

HD = 64
HG = 2
SUB = 16
CAP = 2
TILE = 256
LOWEST = -1e30
LOG2E = math.log2(math.e)
CAST = jnp.bfloat16
TOGETHER = 2


very_negative = -1e30


def from_behind(value, axis, by):
    peers = lax.axis_size(axis)
    pairs = [(i, i + by) for i in range(peers) if 0 <= i + by < peers]
    return lax.ppermute(value, axis, pairs)


def split_heads(values):
    return values.reshape(values.shape[0], values.shape[1] // HD, HD)


def forward_group(query_part, key_part, value_part, key_mask, scaling):
    scores = (
        jnp.einsum(
            "qhd,khd->hqk",
            split_heads(query_part),
            split_heads(key_part),
            preferred_element_type=jnp.float32,
        )
        * scaling
    )
    scores = jnp.where(key_mask[None], scores, very_negative)
    weights = jax.nn.softmax(scores, axis=-1)
    weights_low = weights.astype(jnp.bfloat16)
    mixed_heads = jnp.einsum(
        "hqk,khd->qhd", weights_low, split_heads(value_part), preferred_element_type=jnp.float32
    )
    mixed_part = mixed_heads.reshape(query_part.shape).astype(jnp.bfloat16)
    return (weights, weights_low, mixed_part)


def backward_group(
    query_part, key_part, value_part, grad_part, mixed_part, weights, weights_low, scaling
):
    grad_heads = split_heads(grad_part)
    row_delta = jnp.sum(
        grad_heads.astype(jnp.float32) * split_heads(mixed_part).astype(jnp.float32), axis=-1
    )
    row_delta = jnp.transpose(row_delta)[:, :, None]
    weight_grads = jnp.einsum(
        "qhd,khd->hqk", grad_heads, split_heads(value_part), preferred_element_type=jnp.float32
    )
    score_grads = (weights * (weight_grads - row_delta)).astype(jnp.bfloat16)
    query_grads = (
        jnp.einsum(
            "hqk,khd->qhd", score_grads, split_heads(key_part), preferred_element_type=jnp.float32
        )
        * scaling
    )
    key_grads = (
        jnp.einsum(
            "hqk,qhd->khd", score_grads, split_heads(query_part), preferred_element_type=jnp.float32
        )
        * scaling
    )
    value_grads = jnp.einsum(
        "hqk,qhd->khd", weights_low, grad_heads, preferred_element_type=jnp.float32
    )
    return (
        query_grads.reshape(query_part.shape),
        key_grads.reshape(key_part.shape),
        value_grads.reshape(key_part.shape),
    )


def block_plan(queries, key_rows, value_rows, grad_output, extra_blocks):
    devices = lax.axis_size("tm")
    position = lax.axis_index("tm")
    block_rows = queries.shape[0]
    model_width = queries.shape[1]
    per_block = block_rows // SUB
    group_width = HG * HD
    group_count = model_width // group_width
    scaling = 1.0 / math.sqrt(HD)
    distances = []
    reach = 1
    while reach < devices:
        distances.append(reach)
        reach = reach * 2
    key_value = jnp.concatenate([key_rows, value_rows], axis=1)
    partner_blocks = [from_behind(key_value, "tm", distance) for distance in distances]
    owner_table = jnp.where(extra_blocks >= 0, extra_blocks // per_block, -1)
    inside_table = jnp.where(extra_blocks >= 0, extra_blocks % per_block, 0)
    owned_here = owner_table == position
    ranked = jnp.cumsum(owned_here.astype(jnp.int32), axis=1) - 1
    slot_ids = jnp.arange(CAP, dtype=jnp.int32)
    chosen = owned_here[:, None, :] & (ranked[:, None, :] == slot_ids[None, :, None])
    send_valid = jnp.any(chosen, axis=2)
    send_index = jnp.sum(jnp.where(chosen, inside_table[:, None, :], 0), axis=2)
    key_value_subs = key_value.reshape(per_block, SUB * 2 * model_width)
    send_rows = jnp.take(key_value_subs, send_index.reshape(-1), axis=0).reshape(
        devices * CAP * SUB, 2 * model_width
    )
    extra_rows = lax.all_to_all(send_rows, "tm", split_axis=0, concat_axis=0, tiled=True)
    my_owners = lax.dynamic_index_in_dim(owner_table, position, 0, keepdims=False)
    owner_ids = jnp.arange(devices, dtype=jnp.int32)
    taken_count = jnp.sum((my_owners[None, :] == owner_ids[:, None]).astype(jnp.int32), axis=1)
    slot_live = taken_count[:, None] > slot_ids[None, :]
    extra_live = jnp.repeat(slot_live.reshape(-1), SUB)
    row_ids = jnp.arange(block_rows, dtype=jnp.int32)
    own_mask = row_ids[:, None] >= row_ids[None, :]
    partner_live = jnp.concatenate(
        [jnp.broadcast_to(position >= distance, (block_rows,)) for distance in distances]
    )
    far_live = jnp.concatenate([partner_live, extra_live])
    key_mask = jnp.concatenate(
        [own_mask, jnp.broadcast_to(far_live[None, :], (block_rows, far_live.shape[0]))], axis=1
    )
    all_keys = jnp.concatenate([key_value] + partner_blocks + [extra_rows], axis=0)

    def columns(array, group_index, offset):
        return array[
            :, offset + group_index * group_width : offset + (group_index + 1) * group_width
        ]

    mixed_parts, query_parts, key_parts, value_parts = ([], [], [], [])
    for group_index in range(group_count):
        query_part = columns(queries, group_index, 0)
        key_part = columns(all_keys, group_index, 0)
        value_part = columns(all_keys, group_index, model_width)
        weights, weights_low, mixed_part = forward_group(
            query_part, key_part, value_part, key_mask, scaling
        )
        mixed_parts.append(mixed_part)
        grads = backward_group(
            query_part,
            key_part,
            value_part,
            columns(grad_output, group_index, 0),
            mixed_part,
            weights,
            weights_low,
            scaling,
        )
        query_parts.append(grads[0])
        key_parts.append(grads[1])
        value_parts.append(grads[2])
    mixed_rows = jnp.concatenate(mixed_parts, axis=1)
    query_grad = jnp.concatenate(query_parts, axis=1).astype(jnp.bfloat16)
    grads_all = jnp.concatenate(
        [jnp.concatenate(key_parts, axis=1), jnp.concatenate(value_parts, axis=1)], axis=1
    )
    grad_total = grads_all[:block_rows]
    partner_terms = [
        grads_all[(1 + level) * block_rows : (2 + level) * block_rows]
        for level in range(len(distances))
    ]
    extra_terms = grads_all[(1 + len(distances)) * block_rows :]
    for level, distance in enumerate(distances):
        returned = from_behind(partner_terms[level].astype(jnp.bfloat16), "tm", -distance)
        grad_total = grad_total + returned.astype(jnp.float32)
    extra_back = lax.all_to_all(
        extra_terms.astype(jnp.bfloat16), "tm", split_axis=0, concat_axis=0, tiled=True
    )
    sub_ids = jnp.arange(per_block, dtype=jnp.int32)
    one_hot = (
        (send_index.reshape(-1)[None, :] == sub_ids[:, None]) & send_valid.reshape(-1)[None, :]
    ).astype(jnp.bfloat16)
    folded = jnp.dot(
        one_hot,
        extra_back.reshape(devices * CAP, SUB * 2 * model_width),
        preferred_element_type=jnp.float32,
    )
    grad_total = grad_total + folded.reshape(block_rows, 2 * model_width)
    key_grad = grad_total[:, :model_width].astype(jnp.bfloat16)
    value_grad = grad_total[:, model_width:].astype(jnp.bfloat16)
    return (mixed_rows, query_grad, key_grad, value_grad)


def nn(a, b):
    return lax.dot_general(a, b, (((1,), (0,)), ((), ())), preferred_element_type=jnp.float32)


def by_eights(x, op):
    parts = [x[i : i + 8] for i in range(0, x.shape[0], 8)]
    while len(parts) > 1:
        parts = [op(*parts[i : i + 2]) if i + 1 < len(parts) else parts[i] for i in range(0, len(parts), 2)]
    return parts[0]


def wrapped(i, count):
    return jnp.where(i < 0, i + count, jnp.where(i >= count, i - count, i))


def in_turn(*steps):
    steps = list(steps)
    while steps:
        for step in list(steps):
            if next(step, steps) is steps:
                steps.remove(step)


class Block:
    def __init__(self, b, partners, rows, first_query, table, kv, kv_t, block, scores, gathered, sg, wl, dacc, oq):
        self.oq = oq
        self.kv, self.kv_t, self.scores, self.gathered, self.dacc, self.b = kv, kv_t, scores, gathered, dacc, b
        self.sg, self.wl = sg, wl
        self.queries = queries = block.shape[0]
        width = 2 * HD
        scaling = 1.0 / math.sqrt(HD)
        lane = lax.broadcasted_iota(jnp.int32, block.shape, 1)
        zero = jnp.zeros_like(block)
        q_part = jnp.where(lane < HD, block * CAST(scaling), zero)
        g_part = jnp.where(lane < HD, zero, block)
        self.qg_part = jnp.concatenate([q_part, g_part], axis=0)
        self.block_t = jnp.transpose(block.astype(jnp.float32))
        row_t = lax.broadcasted_iota(jnp.int32, (width, queries), 0)
        self.q_t = jnp.where(row_t < HD, self.block_t * scaling, 0.0).astype(CAST)
        self.g_t = jnp.where(row_t < HD, 0.0, self.block_t).astype(CAST)
        self.chunks = []
        if first_query:
            self.chunks.append((b, 0, first_query, "all"))
        self.chunks.append((b, first_query, queries, "own"))
        for p in range(partners):
            self.chunks.append((b - (1 << p), 0, rows, "all"))
        self.extra_places = []
        entries = min(table.shape[1], CAP * ((1 << partners) - 1))
        if partners:
            self.live = jnp.int32(0)
            for e in range(entries):
                entry = table[b, e]
                self.live = self.live + (entry >= 0).astype(jnp.int32)
                entry = jnp.maximum(entry, 0)
                place = (entry // (rows // SUB), pl.multiple_of(entry % (rows // SUB) * SUB, SUB))
                self.extra_places.append(place)
                gathered[e * SUB : (e + 1) * SUB, :] = kv[place[0], pl.ds(place[1], SUB), :]
            self.gathered_t = jnp.transpose(gathered[: entries * SUB, :])
            self.chunks.append((None, 0, entries * SUB, "extra"))
        self.places = []
        at = 0
        for chunk in self.chunks:
            self.places.append(slice(at, at + chunk[2]))
            at += chunk[2]

    def keys(self, chunk):
        block, first, count, kind = chunk
        if kind == "extra":
            return self.gathered[:count, :]
        return self.kv[block, first : first + count, :]

    def keys_t(self, chunk):
        block, first, count, kind = chunk
        if kind == "extra":
            return self.gathered_t
        return self.kv_t[block, :, first : first + count]

    def score(self):
        peak = jnp.full((8, self.queries), LOWEST, jnp.float32)
        for chunk, place in zip(self.chunks, self.places):
            s = nn(self.keys(chunk), self.q_t) * LOG2E
            row = lax.broadcasted_iota(jnp.int32, s.shape, 0)
            if chunk[3] == "own":
                s = jnp.where(row <= lax.broadcasted_iota(jnp.int32, s.shape, 1), s, LOWEST)
            if chunk[3] == "extra":
                s = jnp.where(row < self.live * SUB, s, LOWEST)
            self.scores[place, :] = s
            peak = jnp.maximum(peak, by_eights(s, jnp.maximum))
            yield
        self.top = jnp.max(peak, axis=0, keepdims=True)

    def mix(self):
        total = jnp.zeros((8, self.queries), jnp.float32)
        mixed = jnp.zeros((HD, self.queries), jnp.float32)
        for chunk, place in zip(self.chunks, self.places):
            w = jnp.exp2(self.scores[place, :] - self.top)
            total = total + by_eights(w, jnp.add)
            mixed = mixed + nn(self.keys_t(chunk)[HD:], w.astype(CAST))
            yield
        total = jnp.sum(total, axis=0, keepdims=True)
        self.mixed = mixed / total
        low = self.mixed.astype(CAST).astype(jnp.float32)
        self.delta = jnp.sum(self.block_t[HD:] * low, axis=0, keepdims=True)
        self.norm = self.top + jnp.log(total) * LOG2E

    def factors(self):
        for chunk, place in zip(self.chunks, self.places):
            w = jnp.exp2(self.scores[place, :] - self.norm)
            self.sg[place, :] = (w * (nn(self.keys(chunk), self.g_t) - self.delta)).astype(CAST)
            self.wl[place, :] = w.astype(CAST)
            yield

    def products(self):
        query_grad = jnp.zeros((HD, self.queries), jnp.float32)
        for chunk, place in zip(self.chunks, self.places):
            sg = self.sg[place, :]
            query_grad = query_grad + nn(self.keys_t(chunk)[:HD], sg)
            part = nn(jnp.concatenate([sg, self.wl[place, :]], axis=1), self.qg_part)
            block, first, count, kind = chunk
            if kind == "extra":
                for e, (owner, at) in enumerate(self.extra_places):
                    self.dacc[owner, pl.ds(at, SUB), :] += part[e * SUB : (e + 1) * SUB]
            else:
                self.dacc[block, first : first + count, :] += part
            yield
        both = jnp.concatenate([query_grad * (1.0 / math.sqrt(HD)), self.mixed], axis=0)
        self.oq[self.b] = jnp.transpose(both).astype(CAST)


def attention_kernel(blocks, rows, first_query, queries, together, *refs):
    last = first_query + queries == rows
    refs = list(refs)

    def take(n):
        got = refs[:n]
        del refs[:n]
        return got

    me_ref, table = take(2)
    early = take(blocks)
    me = me_ref[0]
    if last:
        qd, sums = take(2)
        out = take(blocks)
        kv, kv_t, scores, gathered, sg, wl, dacc, held, moved, oq = take(10)
        for b in range(blocks):
            pltpu.make_async_copy(sums.at[b], held.at[b], moved.at[b]).start()
    else:
        oq, sums, kv, kv_t, scores, gathered, sg, wl, dacc, held, moved, qd = take(12)
    dacc[...] = jnp.zeros_like(dacc)
    for k in range(blocks):
        b = wrapped(me - k, blocks)
        keys = early[k][:rows, :]
        kv[b] = keys
        kv_t[b] = jnp.transpose(keys)
        if not last:
            qd[b] = early[k][rows:, :]
    levels = (blocks - 1).bit_length()

    def run(partners, ids):
        work = [
            Block(b, partners, rows, first_query, table, kv, kv_t, qd[b], scores.at[i], gathered.at[i], sg.at[i],
                  wl.at[i], dacc, oq)
            for i, b in enumerate(ids)
        ]
        for w in work:
            in_turn(w.score())
        for w in work:
            in_turn(w.mix())
        in_turn(work[0].factors())
        for now, then in zip(work, work[1:] + [None]):
            if then:
                in_turn(then.factors(), now.products())
            else:
                in_turn(now.products())
        if not last:
            for w in work:
                held[w.b] = dacc[w.b]
                pltpu.make_async_copy(held.at[w.b], sums.at[w.b], moved.at[w.b]).start()

    for partners in range(levels, -1, -1):
        low = (1 << partners) >> 1
        high = min(1 << partners, blocks)
        group = math.gcd(together, high - low)

        def step(i, carry, partners=partners, high=high, group=group):
            run(partners, [high - 1 - i * group - j for j in range(group)])
            return carry

        if high - low > group:
            lax.fori_loop(0, (high - low) // group, step, 0)
        else:
            run(partners, [jnp.int32(high - 1 - j) for j in range(group)])
    for b in range(blocks):
        if last:
            pltpu.make_async_copy(sums.at[b], held.at[b], moved.at[b]).wait()
        else:
            pltpu.make_async_copy(held.at[b], sums.at[b], moved.at[b]).wait()
    if last:
        for k in range(blocks):
            b = wrapped(me + k, blocks)
            out[k][:rows, :] = (dacc[b] + held[b]).astype(CAST)
            out[k][rows:, :] = oq[b]


def attention(me, table, early, late, before, rows, first_query, queries, together=None):
    together = TOGETHER if together is None else together
    blocks = len(early)
    width = early[0].shape[1]
    entries = table.shape[1]
    levels = (blocks - 1).bit_length()
    last = first_query + queries == rows
    whole = pl.BlockSpec(memory_space=pltpu.VMEM)
    small = pl.BlockSpec(memory_space=pltpu.SMEM)
    apart = pl.BlockSpec(memory_space=pltpu.HBM)
    sums = (blocks, rows, width)
    if last:
        out_shape = [jax.ShapeDtypeStruct((rows + queries, width), CAST)] * blocks
        before = pltpu.with_memory_space_constraint(before, pltpu.HBM)
        inputs = [me, table] + list(early) + [late, before]
    else:
        out_shape = [jax.ShapeDtypeStruct((blocks, queries, width), CAST), pltpu.HBM(sums, jnp.float32)]
        inputs = [me, table] + list(early)
    extra_rows = min(entries, CAP * ((1 << levels) - 1)) * SUB
    list_rows = first_query + queries + levels * rows + extra_rows
    scratch = [
        pltpu.VMEM((blocks, rows, width), CAST),
        pltpu.VMEM((blocks, width, rows), CAST),
        pltpu.VMEM((together, list_rows, queries), jnp.float32),
        pltpu.VMEM((together, extra_rows, width), CAST),
        pltpu.VMEM((together, list_rows, queries), CAST),
        pltpu.VMEM((together, list_rows, queries), CAST),
    ]
    scratch += [pltpu.VMEM(sums, jnp.float32)] * 2 + [pltpu.SemaphoreType.DMA((blocks,))]
    scratch.append(pltpu.VMEM((blocks, queries, width), CAST))
    pairs = blocks * (levels + 1) * rows * queries
    return pl.pallas_call(
        functools.partial(attention_kernel, blocks, rows, first_query, queries, together),
        out_shape=tuple(out_shape),
        in_specs=[small] * 2 + [whole] * (len(inputs) - 3) + [apart if last else whole],
        out_specs=(whole,) * (len(out_shape) - 1) + (whole if last else apart,),
        scratch_shapes=scratch,
        cost_estimate=pl.CostEstimate(flops=pairs * HD * 2 * 6 * 4, transcendentals=2 * pairs, bytes_accessed=8 << 20),
        compiler_params=pltpu.CompilerParams(vmem_limit_bytes=30 * 1024 * 1024),
    )(*inputs)


def swap(x):
    return jnp.concatenate([x[:, HD:], x[:, :HD]], axis=1)


def interleave(first, second):
    lane = lax.broadcasted_iota(jnp.int32, first.shape, 1)
    return jnp.where(lane < HD, first, swap(second)), jnp.where(lane < HD, swap(first), second)


def pack_kernel(heads, pieces, apart, count, *refs):
    me = refs[0][0]
    sources, results = refs[1 : 1 + count], refs[1 + count : -3]
    packed, inputs, arrived = refs[-3:]
    rows = sources[0].shape[0]
    parts = 2

    def copy(i, part):
        place = pl.ds(part * (rows // parts), rows // parts)
        return pltpu.make_async_copy(sources[i].at[place], inputs.at[i, place], arrived.at[i * parts + part])

    for i in range(count):
        for part in range(parts):
            copy(i, part).start()
    ready = set()
    at = 0
    for first, second, low, size in pieces:
        for i in (first, second):
            if i not in ready:
                for part in range(parts):
                    copy(i, part).wait()
                ready.add(i)
        for pair in range(heads // 2):
            lanes = slice(pair * 2 * HD, (pair + 1) * 2 * HD)
            both = interleave(inputs[first, low : low + size, lanes], inputs[second, low : low + size, lanes])
            packed[2 * pair, at : at + size, :] = both[0]
            packed[2 * pair + 1, at : at + size, :] = both[1]
        at += size
    if apart:
        for k, out in enumerate(results):
            out[...] = packed[wrapped(me + k, heads)]
    else:
        results[0][...] = packed[...]


def pack(me, arrays, pieces, apart):
    rows, columns = arrays[0].shape
    heads = columns // HD
    total = sum(piece[3] for piece in pieces)
    whole = pl.BlockSpec(memory_space=pltpu.VMEM)
    all_heads = (heads, total, 2 * HD)
    if apart:
        out_shape = (jax.ShapeDtypeStruct((total, 2 * HD), CAST),) * heads
        out_specs = (whole,) * heads
    else:
        out_shape, out_specs = jax.ShapeDtypeStruct(all_heads, CAST), whole
    return pl.pallas_call(
        functools.partial(pack_kernel, heads, pieces, apart, len(arrays)),
        out_shape=out_shape,
        in_specs=[pl.BlockSpec(memory_space=pltpu.SMEM)] + [pl.BlockSpec(memory_space=pltpu.HBM)] * len(arrays),
        out_specs=out_specs,
        scratch_shapes=[
            pltpu.VMEM(all_heads, CAST),
            pltpu.VMEM((len(arrays), rows, columns), CAST),
            pltpu.SemaphoreType.DMA((2 * len(arrays),)),
        ],
        compiler_params=pltpu.CompilerParams(vmem_limit_bytes=12 * 1024 * 1024),
        cost_estimate=pl.CostEstimate(flops=0, transcendentals=0, bytes_accessed=8 * total * heads * HD),
    )(me, *[pltpu.with_memory_space_constraint(array, pltpu.HBM) for array in arrays])


def unpack_kernel(heads, rows, *refs):
    me = refs[0][0]
    early, late = refs[1], refs[2 : 2 + heads]
    mixed, query_grad, key_grad, value_grad, ordered = refs[2 + heads :]
    for k in range(heads):
        ordered[wrapped(me - k, heads)] = late[k][...]
    half = early.shape[1]
    for pair in range(heads // 2):
        lanes = slice(pair * 2 * HD, (pair + 1) * 2 * HD)
        even, odd = ordered[2 * pair], ordered[2 * pair + 1]
        query_grad[:half, lanes], mixed[:half, lanes] = interleave(early[2 * pair], early[2 * pair + 1])
        query_grad[half:, lanes], mixed[half:, lanes] = interleave(even[rows:], odd[rows:])
        key_grad[:, lanes], value_grad[:, lanes] = interleave(even[:rows], odd[:rows])


def unpack(me, early, late, rows):
    heads = len(late)
    whole = pl.BlockSpec(memory_space=pltpu.VMEM)
    return pl.pallas_call(
        functools.partial(unpack_kernel, heads, rows),
        out_shape=(jax.ShapeDtypeStruct((rows, heads * HD), CAST),) * 4,
        in_specs=[pl.BlockSpec(memory_space=pltpu.SMEM)] + [whole] * (1 + heads),
        out_specs=(whole,) * 4,
        scratch_shapes=[pltpu.VMEM((heads,) + late[0].shape, CAST)],
        compiler_params=pltpu.CompilerParams(vmem_limit_bytes=10 * 1024 * 1024),
    )(me, early, *late)


def shifted_all(pieces):
    count = len(pieces)
    got = {0: pieces[0]}
    for k in sorted(range(1, count), key=lambda k: k):
        got[k] = lax.ppermute(pieces[k], "tm", [(i, (i + k) % count) for i in range(count)])
    return [got[k] for k in range(count)]


def all_heads(packed):
    return lax.all_to_all(packed, "tm", split_axis=0, concat_axis=0, tiled=True)


def head_plan(queries, key_rows, value_rows, grad_output, extra_blocks):
    rows = queries.shape[0]
    half = rows // 2
    me = lax.axis_index("tm").astype(jnp.int32).reshape(1)
    early = shifted_all(
        pack(me, (key_rows, value_rows, queries, grad_output), ((0, 1, 0, rows), (2, 3, 0, half)), True)
    )
    late_packed = pack(me, (queries, grad_output), ((0, 1, half, half),), False)
    *early, late_packed = lax.optimization_barrier((*early, late_packed))
    late = all_heads(late_packed)
    early_rows, sums = attention(me, extra_blocks, early, None, None, rows, 0, half)
    early_back = all_heads(early_rows)
    late_rows = attention(me, extra_blocks, early, late, sums, rows, half, half)
    late_back = shifted_all(late_rows)
    return unpack(me, early_back, late_back, rows)


def local(queries, key_rows, value_rows, grad_output, extra_blocks):
    if lax.axis_size("tm") == queries.shape[1] // HD:
        return head_plan(queries, key_rows, value_rows, grad_output, extra_blocks)
    return block_plan(queries, key_rows, value_rows, grad_output, extra_blocks)


def solution(mesh):
    placed = (
        P(("member", "tm"), None),
        P(("member", "tm"), None),
        P(("member", "tm"), None),
        P(("member", "tm"), None),
        P("member", None),
    )
    return jax.shard_map(
        local,
        mesh=mesh,
        in_specs=placed,
        out_specs=(
            P(("member", "tm"), None),
            P(("member", "tm"), None),
            P(("member", "tm"), None),
            P(("member", "tm"), None),
        ),
        check_vma=False,
    )
```

```python
import functools
import math

import jax
import jax.numpy as jnp
from jax import lax
from jax.experimental import pallas as pl
from jax.experimental.pallas import tpu as pltpu
from jax.sharding import PartitionSpec as P

HD = 64
HG = 2
SUB = 16
CAP = 2
TILE = 256
LOWEST = -1e30
LOG2E = math.log2(math.e)
CAST = jnp.bfloat16
TOGETHER = 2


very_negative = -1e30


def from_behind(value, axis, by):
    peers = lax.axis_size(axis)
    pairs = [(i, i + by) for i in range(peers) if 0 <= i + by < peers]
    return lax.ppermute(value, axis, pairs)


def split_heads(values):
    return values.reshape(values.shape[0], values.shape[1] // HD, HD)


def forward_group(query_part, key_part, value_part, key_mask, scaling):
    scores = (
        jnp.einsum(
            "qhd,khd->hqk",
            split_heads(query_part),
            split_heads(key_part),
            preferred_element_type=jnp.float32,
        )
        * scaling
    )
    scores = jnp.where(key_mask[None], scores, very_negative)
    weights = jax.nn.softmax(scores, axis=-1)
    weights_low = weights.astype(jnp.bfloat16)
    mixed_heads = jnp.einsum(
        "hqk,khd->qhd", weights_low, split_heads(value_part), preferred_element_type=jnp.float32
    )
    mixed_part = mixed_heads.reshape(query_part.shape).astype(jnp.bfloat16)
    return (weights, weights_low, mixed_part)


def backward_group(
    query_part, key_part, value_part, grad_part, mixed_part, weights, weights_low, scaling
):
    grad_heads = split_heads(grad_part)
    row_delta = jnp.sum(
        grad_heads.astype(jnp.float32) * split_heads(mixed_part).astype(jnp.float32), axis=-1
    )
    row_delta = jnp.transpose(row_delta)[:, :, None]
    weight_grads = jnp.einsum(
        "qhd,khd->hqk", grad_heads, split_heads(value_part), preferred_element_type=jnp.float32
    )
    score_grads = (weights * (weight_grads - row_delta)).astype(jnp.bfloat16)
    query_grads = (
        jnp.einsum(
            "hqk,khd->qhd", score_grads, split_heads(key_part), preferred_element_type=jnp.float32
        )
        * scaling
    )
    key_grads = (
        jnp.einsum(
            "hqk,qhd->khd", score_grads, split_heads(query_part), preferred_element_type=jnp.float32
        )
        * scaling
    )
    value_grads = jnp.einsum(
        "hqk,qhd->khd", weights_low, grad_heads, preferred_element_type=jnp.float32
    )
    return (
        query_grads.reshape(query_part.shape),
        key_grads.reshape(key_part.shape),
        value_grads.reshape(key_part.shape),
    )


def block_plan(queries, key_rows, value_rows, grad_output, extra_blocks):
    devices = lax.axis_size("tm")
    position = lax.axis_index("tm")
    block_rows = queries.shape[0]
    model_width = queries.shape[1]
    per_block = block_rows // SUB
    group_width = HG * HD
    group_count = model_width // group_width
    scaling = 1.0 / math.sqrt(HD)
    distances = []
    reach = 1
    while reach < devices:
        distances.append(reach)
        reach = reach * 2
    key_value = jnp.concatenate([key_rows, value_rows], axis=1)
    partner_blocks = [from_behind(key_value, "tm", distance) for distance in distances]
    owner_table = jnp.where(extra_blocks >= 0, extra_blocks // per_block, -1)
    inside_table = jnp.where(extra_blocks >= 0, extra_blocks % per_block, 0)
    owned_here = owner_table == position
    ranked = jnp.cumsum(owned_here.astype(jnp.int32), axis=1) - 1
    slot_ids = jnp.arange(CAP, dtype=jnp.int32)
    chosen = owned_here[:, None, :] & (ranked[:, None, :] == slot_ids[None, :, None])
    send_valid = jnp.any(chosen, axis=2)
    send_index = jnp.sum(jnp.where(chosen, inside_table[:, None, :], 0), axis=2)
    key_value_subs = key_value.reshape(per_block, SUB * 2 * model_width)
    send_rows = jnp.take(key_value_subs, send_index.reshape(-1), axis=0).reshape(
        devices * CAP * SUB, 2 * model_width
    )
    extra_rows = lax.all_to_all(send_rows, "tm", split_axis=0, concat_axis=0, tiled=True)
    my_owners = lax.dynamic_index_in_dim(owner_table, position, 0, keepdims=False)
    owner_ids = jnp.arange(devices, dtype=jnp.int32)
    taken_count = jnp.sum((my_owners[None, :] == owner_ids[:, None]).astype(jnp.int32), axis=1)
    slot_live = taken_count[:, None] > slot_ids[None, :]
    extra_live = jnp.repeat(slot_live.reshape(-1), SUB)
    row_ids = jnp.arange(block_rows, dtype=jnp.int32)
    own_mask = row_ids[:, None] >= row_ids[None, :]
    partner_live = jnp.concatenate(
        [jnp.broadcast_to(position >= distance, (block_rows,)) for distance in distances]
    )
    far_live = jnp.concatenate([partner_live, extra_live])
    key_mask = jnp.concatenate(
        [own_mask, jnp.broadcast_to(far_live[None, :], (block_rows, far_live.shape[0]))], axis=1
    )
    all_keys = jnp.concatenate([key_value] + partner_blocks + [extra_rows], axis=0)

    def columns(array, group_index, offset):
        return array[
            :, offset + group_index * group_width : offset + (group_index + 1) * group_width
        ]

    mixed_parts, query_parts, key_parts, value_parts = ([], [], [], [])
    for group_index in range(group_count):
        query_part = columns(queries, group_index, 0)
        key_part = columns(all_keys, group_index, 0)
        value_part = columns(all_keys, group_index, model_width)
        weights, weights_low, mixed_part = forward_group(
            query_part, key_part, value_part, key_mask, scaling
        )
        mixed_parts.append(mixed_part)
        grads = backward_group(
            query_part,
            key_part,
            value_part,
            columns(grad_output, group_index, 0),
            mixed_part,
            weights,
            weights_low,
            scaling,
        )
        query_parts.append(grads[0])
        key_parts.append(grads[1])
        value_parts.append(grads[2])
    mixed_rows = jnp.concatenate(mixed_parts, axis=1)
    query_grad = jnp.concatenate(query_parts, axis=1).astype(jnp.bfloat16)
    grads_all = jnp.concatenate(
        [jnp.concatenate(key_parts, axis=1), jnp.concatenate(value_parts, axis=1)], axis=1
    )
    grad_total = grads_all[:block_rows]
    partner_terms = [
        grads_all[(1 + level) * block_rows : (2 + level) * block_rows]
        for level in range(len(distances))
    ]
    extra_terms = grads_all[(1 + len(distances)) * block_rows :]
    for level, distance in enumerate(distances):
        returned = from_behind(partner_terms[level].astype(jnp.bfloat16), "tm", -distance)
        grad_total = grad_total + returned.astype(jnp.float32)
    extra_back = lax.all_to_all(
        extra_terms.astype(jnp.bfloat16), "tm", split_axis=0, concat_axis=0, tiled=True
    )
    sub_ids = jnp.arange(per_block, dtype=jnp.int32)
    one_hot = (
        (send_index.reshape(-1)[None, :] == sub_ids[:, None]) & send_valid.reshape(-1)[None, :]
    ).astype(jnp.bfloat16)
    folded = jnp.dot(
        one_hot,
        extra_back.reshape(devices * CAP, SUB * 2 * model_width),
        preferred_element_type=jnp.float32,
    )
    grad_total = grad_total + folded.reshape(block_rows, 2 * model_width)
    key_grad = grad_total[:, :model_width].astype(jnp.bfloat16)
    value_grad = grad_total[:, model_width:].astype(jnp.bfloat16)
    return (mixed_rows, query_grad, key_grad, value_grad)


def nn(a, b):
    return lax.dot_general(a, b, (((1,), (0,)), ((), ())), preferred_element_type=jnp.float32)


def by_eights(x, op):
    parts = [x[i : i + 8] for i in range(0, x.shape[0], 8)]
    while len(parts) > 1:
        parts = [op(*parts[i : i + 2]) if i + 1 < len(parts) else parts[i] for i in range(0, len(parts), 2)]
    return parts[0]


def wrapped(i, count):
    return jnp.where(i < 0, i + count, jnp.where(i >= count, i - count, i))


def in_turn(*steps):
    steps = list(steps)
    while steps:
        for step in list(steps):
            if next(step, steps) is steps:
                steps.remove(step)


def tn(a, b):
    return lax.dot_general(a, b, (((0,), (0,)), ((), ())), preferred_element_type=jnp.float32)


class Block:
    def __init__(self, b, partners, rows, first_query, table, kv, block, scores, gathered, sg, wl, dacc, oq):
        self.oq = oq
        self.kv, self.scores, self.gathered, self.dacc, self.b = kv, scores, gathered, dacc, b
        self.sg, self.wl = sg, wl
        self.queries = queries = block.shape[0]
        width = 2 * HD
        scaling = 1.0 / math.sqrt(HD)
        lane = lax.broadcasted_iota(jnp.int32, block.shape, 1)
        zero = jnp.zeros_like(block)
        q_part = jnp.where(lane < HD, block * CAST(scaling), zero)
        g_part = jnp.where(lane < HD, zero, block)
        self.qg_part = jnp.concatenate([q_part, g_part], axis=0)
        self.block_t = jnp.transpose(block.astype(jnp.float32))
        row_t = lax.broadcasted_iota(jnp.int32, (width, queries), 0)
        self.q_t = jnp.where(row_t < HD, self.block_t * scaling, 0.0).astype(CAST)
        self.g_t = jnp.where(row_t < HD, 0.0, self.block_t).astype(CAST)
        self.chunks = []
        if first_query:
            self.chunks.append((b, 0, first_query, "all"))
        self.chunks.append((b, first_query, queries, "own"))
        for p in range(partners):
            self.chunks.append((b - (1 << p), 0, rows, "all"))
        self.extra_places = []
        entries = min(table.shape[1], CAP * ((1 << partners) - 1))
        if partners:
            self.live = jnp.int32(0)
            for e in range(entries):
                entry = table[b, e]
                self.live = self.live + (entry >= 0).astype(jnp.int32)
                entry = jnp.maximum(entry, 0)
                place = (entry // (rows // SUB), pl.multiple_of(entry % (rows // SUB) * SUB, SUB))
                self.extra_places.append(place)
                gathered[e * SUB : (e + 1) * SUB, :] = kv[place[0], pl.ds(place[1], SUB), :]
            self.chunks.append((None, 0, entries * SUB, "extra"))
        self.places = []
        at = 0
        for chunk in self.chunks:
            self.places.append(slice(at, at + chunk[2]))
            at += chunk[2]

    def keys(self, chunk):
        block, first, count, kind = chunk
        if kind == "extra":
            return self.gathered[:count, :]
        return self.kv[block, first : first + count, :]

    def score(self):
        peak = jnp.full((8, self.queries), LOWEST, jnp.float32)
        for chunk, place in zip(self.chunks, self.places):
            s = nn(self.keys(chunk), self.q_t) * LOG2E
            row = lax.broadcasted_iota(jnp.int32, s.shape, 0)
            if chunk[3] == "own":
                s = jnp.where(row <= lax.broadcasted_iota(jnp.int32, s.shape, 1), s, LOWEST)
            if chunk[3] == "extra":
                s = jnp.where(row < self.live * SUB, s, LOWEST)
            self.scores[place, :] = s
            peak = jnp.maximum(peak, by_eights(s, jnp.maximum))
            yield
        self.top = jnp.max(peak, axis=0, keepdims=True)

    def mix(self):
        total = jnp.zeros((8, self.queries), jnp.float32)
        mixed = jnp.zeros((HD, self.queries), jnp.float32)
        for chunk, place in zip(self.chunks, self.places):
            w = jnp.exp2(self.scores[place, :] - self.top)
            total = total + by_eights(w, jnp.add)
            mixed = mixed + tn(self.keys(chunk), w.astype(CAST))[HD:]
            yield
        total = jnp.sum(total, axis=0, keepdims=True)
        self.mixed = mixed / total
        low = self.mixed.astype(CAST).astype(jnp.float32)
        self.delta = jnp.sum(self.block_t[HD:] * low, axis=0, keepdims=True)
        self.norm = self.top + jnp.log(total) * LOG2E

    def factors(self):
        for chunk, place in zip(self.chunks, self.places):
            w = jnp.exp2(self.scores[place, :] - self.norm)
            self.sg[place, :] = (w * (nn(self.keys(chunk), self.g_t) - self.delta)).astype(CAST)
            self.wl[place, :] = w.astype(CAST)
            yield

    def products(self):
        query_grad = jnp.zeros((HD, self.queries), jnp.float32)
        for chunk, place in zip(self.chunks, self.places):
            sg = self.sg[place, :]
            query_grad = query_grad + tn(self.keys(chunk), sg)[:HD]
            part = nn(jnp.concatenate([sg, self.wl[place, :]], axis=1), self.qg_part)
            block, first, count, kind = chunk
            if kind == "extra":
                for e, (owner, at) in enumerate(self.extra_places):
                    self.dacc[owner, pl.ds(at, SUB), :] += part[e * SUB : (e + 1) * SUB]
            else:
                self.dacc[block, first : first + count, :] += part
            yield
        both = jnp.concatenate([query_grad * (1.0 / math.sqrt(HD)), self.mixed], axis=0)
        self.oq[self.b] = jnp.transpose(both).astype(CAST)


def attention_kernel(blocks, rows, first_query, queries, together, *refs):
    last = first_query + queries == rows
    refs = list(refs)

    def take(n):
        got = refs[:n]
        del refs[:n]
        return got

    me_ref, table = take(2)
    early = take(blocks)
    me = me_ref[0]
    if last:
        qd, sums = take(2)
        out = take(blocks)
        kv, scores, gathered, sg, wl, dacc, held, moved, oq = take(9)
        for b in range(blocks):
            pltpu.make_async_copy(sums.at[b], held.at[b], moved.at[b]).start()
    else:
        oq, sums, kv, scores, gathered, sg, wl, dacc, held, moved, qd = take(11)
    dacc[...] = jnp.zeros_like(dacc)
    for k in range(blocks):
        b = wrapped(me - k, blocks)
        keys = early[k][:rows, :]
        kv[b] = keys
        if not last:
            qd[b] = early[k][rows:, :]
    levels = (blocks - 1).bit_length()

    def run(partners, ids):
        work = [
            Block(b, partners, rows, first_query, table, kv, qd[b], scores.at[i], gathered.at[i], sg.at[i],
                  wl.at[i], dacc, oq)
            for i, b in enumerate(ids)
        ]
        for w in work:
            in_turn(w.score())
        for w in work:
            in_turn(w.mix())
        in_turn(work[0].factors())
        for now, then in zip(work, work[1:] + [None]):
            if then:
                in_turn(then.factors(), now.products())
            else:
                in_turn(now.products())
        if not last:
            for w in work:
                held[w.b] = dacc[w.b]
                pltpu.make_async_copy(held.at[w.b], sums.at[w.b], moved.at[w.b]).start()

    for partners in range(levels, -1, -1):
        low = (1 << partners) >> 1
        high = min(1 << partners, blocks)
        group = math.gcd(together, high - low)

        def step(i, carry, partners=partners, high=high, group=group):
            run(partners, [high - 1 - i * group - j for j in range(group)])
            return carry

        if high - low > group:
            lax.fori_loop(0, (high - low) // group, step, 0)
        else:
            run(partners, [jnp.int32(high - 1 - j) for j in range(group)])
    for b in range(blocks):
        if last:
            pltpu.make_async_copy(sums.at[b], held.at[b], moved.at[b]).wait()
        else:
            pltpu.make_async_copy(held.at[b], sums.at[b], moved.at[b]).wait()
    if last:
        for k in range(blocks):
            b = wrapped(me + k, blocks)
            out[k][:rows, :] = (dacc[b] + held[b]).astype(CAST)
            out[k][rows:, :] = oq[b]


def attention(me, table, early, late, before, rows, first_query, queries, together=None):
    together = TOGETHER if together is None else together
    blocks = len(early)
    width = early[0].shape[1]
    entries = table.shape[1]
    levels = (blocks - 1).bit_length()
    last = first_query + queries == rows
    whole = pl.BlockSpec(memory_space=pltpu.VMEM)
    small = pl.BlockSpec(memory_space=pltpu.SMEM)
    apart = pl.BlockSpec(memory_space=pltpu.HBM)
    sums = (blocks, rows, width)
    if last:
        out_shape = [jax.ShapeDtypeStruct((rows + queries, width), CAST)] * blocks
        before = pltpu.with_memory_space_constraint(before, pltpu.HBM)
        inputs = [me, table] + list(early) + [late, before]
    else:
        out_shape = [jax.ShapeDtypeStruct((blocks, queries, width), CAST), pltpu.HBM(sums, jnp.float32)]
        inputs = [me, table] + list(early)
    extra_rows = min(entries, CAP * ((1 << levels) - 1)) * SUB
    list_rows = first_query + queries + levels * rows + extra_rows
    scratch = [
        pltpu.VMEM((blocks, rows, width), CAST),
        pltpu.VMEM((together, list_rows, queries), jnp.float32),
        pltpu.VMEM((together, extra_rows, width), CAST),
        pltpu.VMEM((together, list_rows, queries), CAST),
        pltpu.VMEM((together, list_rows, queries), CAST),
    ]
    scratch += [pltpu.VMEM(sums, jnp.float32)] * 2 + [pltpu.SemaphoreType.DMA((blocks,))]
    scratch.append(pltpu.VMEM((blocks, queries, width), CAST))
    pairs = blocks * (levels + 1) * rows * queries
    return pl.pallas_call(
        functools.partial(attention_kernel, blocks, rows, first_query, queries, together),
        out_shape=tuple(out_shape),
        in_specs=[small] * 2 + [whole] * (len(inputs) - 3) + [apart if last else whole],
        out_specs=(whole,) * (len(out_shape) - 1) + (whole if last else apart,),
        scratch_shapes=scratch,
        cost_estimate=pl.CostEstimate(flops=pairs * HD * 2 * 6 * 4, transcendentals=2 * pairs, bytes_accessed=8 << 20),
        compiler_params=pltpu.CompilerParams(vmem_limit_bytes=30 * 1024 * 1024),
    )(*inputs)


def swap(x):
    return jnp.concatenate([x[:, HD:], x[:, :HD]], axis=1)


def interleave(first, second):
    lane = lax.broadcasted_iota(jnp.int32, first.shape, 1)
    return jnp.where(lane < HD, first, swap(second)), jnp.where(lane < HD, swap(first), second)


def pack_kernel(heads, pieces, apart, count, *refs):
    me = refs[0][0]
    sources, results = refs[1 : 1 + count], refs[1 + count : -3]
    packed, inputs, arrived = refs[-3:]
    rows = sources[0].shape[0]
    parts = 2

    def copy(i, part):
        place = pl.ds(part * (rows // parts), rows // parts)
        return pltpu.make_async_copy(sources[i].at[place], inputs.at[i, place], arrived.at[i * parts + part])

    for i in range(count):
        for part in range(parts):
            copy(i, part).start()
    ready = set()
    at = 0
    for first, second, low, size in pieces:
        for i in (first, second):
            if i not in ready:
                for part in range(parts):
                    copy(i, part).wait()
                ready.add(i)
        for pair in range(heads // 2):
            lanes = slice(pair * 2 * HD, (pair + 1) * 2 * HD)
            both = interleave(inputs[first, low : low + size, lanes], inputs[second, low : low + size, lanes])
            packed[2 * pair, at : at + size, :] = both[0]
            packed[2 * pair + 1, at : at + size, :] = both[1]
        at += size
    if apart:
        for k, out in enumerate(results):
            out[...] = packed[wrapped(me + k, heads)]
    else:
        results[0][...] = packed[...]


def pack(me, arrays, pieces, apart):
    rows, columns = arrays[0].shape
    heads = columns // HD
    total = sum(piece[3] for piece in pieces)
    whole = pl.BlockSpec(memory_space=pltpu.VMEM)
    all_heads = (heads, total, 2 * HD)
    if apart:
        out_shape = (jax.ShapeDtypeStruct((total, 2 * HD), CAST),) * heads
        out_specs = (whole,) * heads
    else:
        out_shape, out_specs = jax.ShapeDtypeStruct(all_heads, CAST), whole
    return pl.pallas_call(
        functools.partial(pack_kernel, heads, pieces, apart, len(arrays)),
        out_shape=out_shape,
        in_specs=[pl.BlockSpec(memory_space=pltpu.SMEM)] + [pl.BlockSpec(memory_space=pltpu.HBM)] * len(arrays),
        out_specs=out_specs,
        scratch_shapes=[
            pltpu.VMEM(all_heads, CAST),
            pltpu.VMEM((len(arrays), rows, columns), CAST),
            pltpu.SemaphoreType.DMA((2 * len(arrays),)),
        ],
        compiler_params=pltpu.CompilerParams(vmem_limit_bytes=12 * 1024 * 1024),
        cost_estimate=pl.CostEstimate(flops=0, transcendentals=0, bytes_accessed=8 * total * heads * HD),
    )(me, *[pltpu.with_memory_space_constraint(array, pltpu.HBM) for array in arrays])


def unpack_kernel(heads, rows, *refs):
    me = refs[0][0]
    early, late = refs[1], refs[2 : 2 + heads]
    mixed, query_grad, key_grad, value_grad, ordered = refs[2 + heads :]
    for k in range(heads):
        ordered[wrapped(me - k, heads)] = late[k][...]
    half = early.shape[1]
    for pair in range(heads // 2):
        lanes = slice(pair * 2 * HD, (pair + 1) * 2 * HD)
        even, odd = ordered[2 * pair], ordered[2 * pair + 1]
        query_grad[:half, lanes], mixed[:half, lanes] = interleave(early[2 * pair], early[2 * pair + 1])
        query_grad[half:, lanes], mixed[half:, lanes] = interleave(even[rows:], odd[rows:])
        key_grad[:, lanes], value_grad[:, lanes] = interleave(even[:rows], odd[:rows])


def unpack(me, early, late, rows):
    heads = len(late)
    whole = pl.BlockSpec(memory_space=pltpu.VMEM)
    return pl.pallas_call(
        functools.partial(unpack_kernel, heads, rows),
        out_shape=(jax.ShapeDtypeStruct((rows, heads * HD), CAST),) * 4,
        in_specs=[pl.BlockSpec(memory_space=pltpu.SMEM)] + [whole] * (1 + heads),
        out_specs=(whole,) * 4,
        scratch_shapes=[pltpu.VMEM((heads,) + late[0].shape, CAST)],
        compiler_params=pltpu.CompilerParams(vmem_limit_bytes=10 * 1024 * 1024),
    )(me, early, *late)


def shifted_all(pieces):
    count = len(pieces)
    got = {0: pieces[0]}
    for k in sorted(range(1, count), key=lambda k: k):
        got[k] = lax.ppermute(pieces[k], "tm", [(i, (i + k) % count) for i in range(count)])
    return [got[k] for k in range(count)]


def all_heads(packed):
    return lax.all_to_all(packed, "tm", split_axis=0, concat_axis=0, tiled=True)


def head_plan(queries, key_rows, value_rows, grad_output, extra_blocks):
    rows = queries.shape[0]
    half = rows // 2
    me = lax.axis_index("tm").astype(jnp.int32).reshape(1)
    early = shifted_all(
        pack(me, (key_rows, value_rows, queries, grad_output), ((0, 1, 0, rows), (2, 3, 0, half)), True)
    )
    late_packed = pack(me, (queries, grad_output), ((0, 1, half, half),), False)
    *early, late_packed = lax.optimization_barrier((*early, late_packed))
    late = all_heads(late_packed)
    early_rows, sums = attention(me, extra_blocks, early, None, None, rows, 0, half)
    early_back = all_heads(early_rows)
    late_rows = attention(me, extra_blocks, early, late, sums, rows, half, half)
    late_back = shifted_all(late_rows)
    return unpack(me, early_back, late_back, rows)


def local(queries, key_rows, value_rows, grad_output, extra_blocks):
    if lax.axis_size("tm") == queries.shape[1] // HD:
        return head_plan(queries, key_rows, value_rows, grad_output, extra_blocks)
    return block_plan(queries, key_rows, value_rows, grad_output, extra_blocks)


def solution(mesh):
    placed = (
        P(("member", "tm"), None),
        P(("member", "tm"), None),
        P(("member", "tm"), None),
        P(("member", "tm"), None),
        P("member", None),
    )
    return jax.shard_map(
        local,
        mesh=mesh,
        in_specs=placed,
        out_specs=(
            P(("member", "tm"), None),
            P(("member", "tm"), None),
            P(("member", "tm"), None),
            P(("member", "tm"), None),
        ),
        check_vma=False,
    )
```

```python
import functools
import math

import jax
import jax.numpy as jnp
from jax import lax
from jax.experimental import pallas as pl
from jax.experimental.pallas import tpu as pltpu
from jax.sharding import PartitionSpec as P

HD = 64
HG = 2
SUB = 16
CAP = 2
TILE = 256
LOWEST = -1e30
LOG2E = math.log2(math.e)
CAST = jnp.bfloat16
TOGETHER = 2


very_negative = -1e30


def from_behind(value, axis, by):
    peers = lax.axis_size(axis)
    pairs = [(i, i + by) for i in range(peers) if 0 <= i + by < peers]
    return lax.ppermute(value, axis, pairs)


def split_heads(values):
    return values.reshape(values.shape[0], values.shape[1] // HD, HD)


def forward_group(query_part, key_part, value_part, key_mask, scaling):
    scores = (
        jnp.einsum(
            "qhd,khd->hqk",
            split_heads(query_part),
            split_heads(key_part),
            preferred_element_type=jnp.float32,
        )
        * scaling
    )
    scores = jnp.where(key_mask[None], scores, very_negative)
    weights = jax.nn.softmax(scores, axis=-1)
    weights_low = weights.astype(jnp.bfloat16)
    mixed_heads = jnp.einsum(
        "hqk,khd->qhd", weights_low, split_heads(value_part), preferred_element_type=jnp.float32
    )
    mixed_part = mixed_heads.reshape(query_part.shape).astype(jnp.bfloat16)
    return (weights, weights_low, mixed_part)


def backward_group(
    query_part, key_part, value_part, grad_part, mixed_part, weights, weights_low, scaling
):
    grad_heads = split_heads(grad_part)
    row_delta = jnp.sum(
        grad_heads.astype(jnp.float32) * split_heads(mixed_part).astype(jnp.float32), axis=-1
    )
    row_delta = jnp.transpose(row_delta)[:, :, None]
    weight_grads = jnp.einsum(
        "qhd,khd->hqk", grad_heads, split_heads(value_part), preferred_element_type=jnp.float32
    )
    score_grads = (weights * (weight_grads - row_delta)).astype(jnp.bfloat16)
    query_grads = (
        jnp.einsum(
            "hqk,khd->qhd", score_grads, split_heads(key_part), preferred_element_type=jnp.float32
        )
        * scaling
    )
    key_grads = (
        jnp.einsum(
            "hqk,qhd->khd", score_grads, split_heads(query_part), preferred_element_type=jnp.float32
        )
        * scaling
    )
    value_grads = jnp.einsum(
        "hqk,qhd->khd", weights_low, grad_heads, preferred_element_type=jnp.float32
    )
    return (
        query_grads.reshape(query_part.shape),
        key_grads.reshape(key_part.shape),
        value_grads.reshape(key_part.shape),
    )


def block_plan(queries, key_rows, value_rows, grad_output, extra_blocks):
    devices = lax.axis_size("tm")
    position = lax.axis_index("tm")
    block_rows = queries.shape[0]
    model_width = queries.shape[1]
    per_block = block_rows // SUB
    group_width = HG * HD
    group_count = model_width // group_width
    scaling = 1.0 / math.sqrt(HD)
    distances = []
    reach = 1
    while reach < devices:
        distances.append(reach)
        reach = reach * 2
    key_value = jnp.concatenate([key_rows, value_rows], axis=1)
    partner_blocks = [from_behind(key_value, "tm", distance) for distance in distances]
    owner_table = jnp.where(extra_blocks >= 0, extra_blocks // per_block, -1)
    inside_table = jnp.where(extra_blocks >= 0, extra_blocks % per_block, 0)
    owned_here = owner_table == position
    ranked = jnp.cumsum(owned_here.astype(jnp.int32), axis=1) - 1
    slot_ids = jnp.arange(CAP, dtype=jnp.int32)
    chosen = owned_here[:, None, :] & (ranked[:, None, :] == slot_ids[None, :, None])
    send_valid = jnp.any(chosen, axis=2)
    send_index = jnp.sum(jnp.where(chosen, inside_table[:, None, :], 0), axis=2)
    key_value_subs = key_value.reshape(per_block, SUB * 2 * model_width)
    send_rows = jnp.take(key_value_subs, send_index.reshape(-1), axis=0).reshape(
        devices * CAP * SUB, 2 * model_width
    )
    extra_rows = lax.all_to_all(send_rows, "tm", split_axis=0, concat_axis=0, tiled=True)
    my_owners = lax.dynamic_index_in_dim(owner_table, position, 0, keepdims=False)
    owner_ids = jnp.arange(devices, dtype=jnp.int32)
    taken_count = jnp.sum((my_owners[None, :] == owner_ids[:, None]).astype(jnp.int32), axis=1)
    slot_live = taken_count[:, None] > slot_ids[None, :]
    extra_live = jnp.repeat(slot_live.reshape(-1), SUB)
    row_ids = jnp.arange(block_rows, dtype=jnp.int32)
    own_mask = row_ids[:, None] >= row_ids[None, :]
    partner_live = jnp.concatenate(
        [jnp.broadcast_to(position >= distance, (block_rows,)) for distance in distances]
    )
    far_live = jnp.concatenate([partner_live, extra_live])
    key_mask = jnp.concatenate(
        [own_mask, jnp.broadcast_to(far_live[None, :], (block_rows, far_live.shape[0]))], axis=1
    )
    all_keys = jnp.concatenate([key_value] + partner_blocks + [extra_rows], axis=0)

    def columns(array, group_index, offset):
        return array[
            :, offset + group_index * group_width : offset + (group_index + 1) * group_width
        ]

    mixed_parts, query_parts, key_parts, value_parts = ([], [], [], [])
    for group_index in range(group_count):
        query_part = columns(queries, group_index, 0)
        key_part = columns(all_keys, group_index, 0)
        value_part = columns(all_keys, group_index, model_width)
        weights, weights_low, mixed_part = forward_group(
            query_part, key_part, value_part, key_mask, scaling
        )
        mixed_parts.append(mixed_part)
        grads = backward_group(
            query_part,
            key_part,
            value_part,
            columns(grad_output, group_index, 0),
            mixed_part,
            weights,
            weights_low,
            scaling,
        )
        query_parts.append(grads[0])
        key_parts.append(grads[1])
        value_parts.append(grads[2])
    mixed_rows = jnp.concatenate(mixed_parts, axis=1)
    query_grad = jnp.concatenate(query_parts, axis=1).astype(jnp.bfloat16)
    grads_all = jnp.concatenate(
        [jnp.concatenate(key_parts, axis=1), jnp.concatenate(value_parts, axis=1)], axis=1
    )
    grad_total = grads_all[:block_rows]
    partner_terms = [
        grads_all[(1 + level) * block_rows : (2 + level) * block_rows]
        for level in range(len(distances))
    ]
    extra_terms = grads_all[(1 + len(distances)) * block_rows :]
    for level, distance in enumerate(distances):
        returned = from_behind(partner_terms[level].astype(jnp.bfloat16), "tm", -distance)
        grad_total = grad_total + returned.astype(jnp.float32)
    extra_back = lax.all_to_all(
        extra_terms.astype(jnp.bfloat16), "tm", split_axis=0, concat_axis=0, tiled=True
    )
    sub_ids = jnp.arange(per_block, dtype=jnp.int32)
    one_hot = (
        (send_index.reshape(-1)[None, :] == sub_ids[:, None]) & send_valid.reshape(-1)[None, :]
    ).astype(jnp.bfloat16)
    folded = jnp.dot(
        one_hot,
        extra_back.reshape(devices * CAP, SUB * 2 * model_width),
        preferred_element_type=jnp.float32,
    )
    grad_total = grad_total + folded.reshape(block_rows, 2 * model_width)
    key_grad = grad_total[:, :model_width].astype(jnp.bfloat16)
    value_grad = grad_total[:, model_width:].astype(jnp.bfloat16)
    return (mixed_rows, query_grad, key_grad, value_grad)


def nn(a, b):
    return lax.dot_general(a, b, (((1,), (0,)), ((), ())), preferred_element_type=jnp.float32)


def by_eights(x, op):
    parts = [x[i : i + 8] for i in range(0, x.shape[0], 8)]
    while len(parts) > 1:
        parts = [op(*parts[i : i + 2]) if i + 1 < len(parts) else parts[i] for i in range(0, len(parts), 2)]
    return parts[0]


def wrapped(i, count):
    return jnp.where(i < 0, i + count, jnp.where(i >= count, i - count, i))


def in_turn(*steps):
    steps = list(steps)
    while steps:
        for step in list(steps):
            if next(step, steps) is steps:
                steps.remove(step)


def tn(a, b):
    return lax.dot_general(a, b, (((0,), (0,)), ((), ())), preferred_element_type=jnp.float32)


class Block:
    def __init__(self, b, partners, rows, first_query, table, kv, block, scores, gathered, sg, wl, dacc, oq):
        self.oq = oq
        self.kv, self.scores, self.gathered, self.dacc, self.b = kv, scores, gathered, dacc, b
        self.sg, self.wl = sg, wl
        self.queries = queries = block.shape[0]
        width = 2 * HD
        scaling = 1.0 / math.sqrt(HD)
        lane = lax.broadcasted_iota(jnp.int32, block.shape, 1)
        zero = jnp.zeros_like(block)
        q_part = jnp.where(lane < HD, block * CAST(scaling), zero)
        g_part = jnp.where(lane < HD, zero, block)
        self.qg_part = jnp.concatenate([q_part, g_part], axis=0)
        self.block_t = jnp.transpose(block.astype(jnp.float32))
        row_t = lax.broadcasted_iota(jnp.int32, (width, queries), 0)
        self.q_t = jnp.where(row_t < HD, self.block_t * scaling, 0.0).astype(CAST)
        self.g_t = jnp.where(row_t < HD, 0.0, self.block_t).astype(CAST)
        self.chunks = []
        if first_query:
            self.chunks.append((b, 0, first_query, "all"))
        self.chunks.append((b, first_query, queries, "own"))
        for p in range(partners):
            self.chunks.append((b - (1 << p), 0, rows, "all"))
        self.extra_places = []
        entries = min(table.shape[1], CAP * ((1 << partners) - 1))
        if partners:
            self.live = jnp.int32(0)
            for e in range(entries):
                entry = table[b, e]
                self.live = self.live + (entry >= 0).astype(jnp.int32)
                entry = jnp.maximum(entry, 0)
                place = (entry // (rows // SUB), pl.multiple_of(entry % (rows // SUB) * SUB, SUB))
                self.extra_places.append(place)
                gathered[e * SUB : (e + 1) * SUB, :] = kv[place[0], pl.ds(place[1], SUB), :]
            self.chunks.append((None, 0, entries * SUB, "extra"))
        self.places = []
        at = 0
        for chunk in self.chunks:
            self.places.append(slice(at, at + chunk[2]))
            at += chunk[2]

    def keys(self, chunk):
        block, first, count, kind = chunk
        if kind == "extra":
            return self.gathered[:count, :]
        return self.kv[block, first : first + count, :]

    def score(self):
        peak = jnp.full((8, self.queries), LOWEST, jnp.float32)
        for chunk, place in zip(self.chunks, self.places):
            s = nn(self.keys(chunk), self.q_t) * LOG2E
            row = lax.broadcasted_iota(jnp.int32, s.shape, 0)
            if chunk[3] == "own":
                s = jnp.where(row <= lax.broadcasted_iota(jnp.int32, s.shape, 1), s, LOWEST)
            if chunk[3] == "extra":
                s = jnp.where(row < self.live * SUB, s, LOWEST)
            self.scores[place, :] = s
            peak = jnp.maximum(peak, by_eights(s, jnp.maximum))
            yield
        self.top = jnp.max(peak, axis=0, keepdims=True)

    def mix(self):
        total = jnp.zeros((8, self.queries), jnp.float32)
        mixed = jnp.zeros((HD, self.queries), jnp.float32)
        for chunk, place in zip(self.chunks, self.places):
            w = jnp.exp2(self.scores[place, :] - self.top)
            total = total + by_eights(w, jnp.add)
            mixed = mixed + tn(self.keys(chunk), w.astype(CAST))[HD:]
            yield
        total = jnp.sum(total, axis=0, keepdims=True)
        self.mixed = mixed / total
        low = self.mixed.astype(CAST).astype(jnp.float32)
        self.delta = jnp.sum(self.block_t[HD:] * low, axis=0, keepdims=True)
        self.norm = self.top + jnp.log(total) * LOG2E

    def factors(self):
        for chunk, place in zip(self.chunks, self.places):
            w = jnp.exp2(self.scores[place, :] - self.norm)
            self.sg[place, :] = (w * (nn(self.keys(chunk), self.g_t) - self.delta)).astype(CAST)
            self.wl[place, :] = w.astype(CAST)
            yield

    def products(self):
        query_grad = jnp.zeros((HD, self.queries), jnp.float32)
        for chunk, place in zip(self.chunks, self.places):
            sg = self.sg[place, :]
            query_grad = query_grad + tn(self.keys(chunk), sg)[:HD]
            part = nn(jnp.concatenate([sg, self.wl[place, :]], axis=1), self.qg_part)
            block, first, count, kind = chunk
            if kind == "extra":
                for e, (owner, at) in enumerate(self.extra_places):
                    self.dacc[owner, pl.ds(at, SUB), :] += part[e * SUB : (e + 1) * SUB]
            else:
                self.dacc[block, first : first + count, :] += part
            yield
        both = jnp.concatenate([query_grad * (1.0 / math.sqrt(HD)), self.mixed], axis=0)
        self.oq[self.b] = jnp.transpose(both).astype(CAST)


def attention_kernel(blocks, rows, first_query, queries, together, *refs):
    last = first_query + queries == rows
    refs = list(refs)

    def take(n):
        got = refs[:n]
        del refs[:n]
        return got

    me_ref, table = take(2)
    early = take(blocks)
    me = me_ref[0]
    if last:
        qd, sums = take(2)
        out = take(blocks)
        kv, scores, gathered, sg, wl, dacc, held, moved, oq = take(9)
        for b in range(blocks):
            pltpu.make_async_copy(sums.at[b], held.at[b], moved.at[b]).start()
    else:
        oq, sums, kv, scores, gathered, sg, wl, dacc, held, moved, qd = take(11)
    dacc[...] = jnp.zeros_like(dacc)
    for k in range(blocks):
        b = wrapped(me - k, blocks)
        keys = early[k][:rows, :]
        kv[b] = keys
        if not last:
            qd[b] = early[k][rows:, :]
    levels = (blocks - 1).bit_length()

    def run(partners, ids):
        work = [
            Block(b, partners, rows, first_query, table, kv, qd[b], scores.at[i], gathered.at[i], sg.at[i],
                  wl.at[i], dacc, oq)
            for i, b in enumerate(ids)
        ]
        for w in work:
            in_turn(w.score())
        for w in work:
            in_turn(w.mix())
        in_turn(work[0].factors())
        for now, then in zip(work, work[1:] + [None]):
            if then:
                in_turn(then.factors(), now.products())
            else:
                in_turn(now.products())
        if not last:
            for w in work:
                held[w.b] = dacc[w.b]
                pltpu.make_async_copy(held.at[w.b], sums.at[w.b], moved.at[w.b]).start()

    for partners in range(levels, -1, -1):
        low = (1 << partners) >> 1
        high = min(1 << partners, blocks)
        group = math.gcd(together, high - low)

        def step(i, carry, partners=partners, high=high, group=group):
            run(partners, [high - 1 - i * group - j for j in range(group)])
            return carry

        if high - low > group:
            lax.fori_loop(0, (high - low) // group, step, 0)
        else:
            run(partners, [jnp.int32(high - 1 - j) for j in range(group)])
    for b in range(blocks):
        if last:
            pltpu.make_async_copy(sums.at[b], held.at[b], moved.at[b]).wait()
        else:
            pltpu.make_async_copy(held.at[b], sums.at[b], moved.at[b]).wait()
    if last:
        for k in range(blocks):
            b = wrapped(me + k, blocks)
            out[k][:rows, :] = (dacc[b] + held[b]).astype(CAST)
            out[k][rows:, :] = oq[b]


def attention(me, table, early, late, before, rows, first_query, queries, together=None):
    together = TOGETHER if together is None else together
    blocks = len(early)
    width = early[0].shape[1]
    entries = table.shape[1]
    levels = (blocks - 1).bit_length()
    last = first_query + queries == rows
    whole = pl.BlockSpec(memory_space=pltpu.VMEM)
    small = pl.BlockSpec(memory_space=pltpu.SMEM)
    apart = pl.BlockSpec(memory_space=pltpu.HBM)
    sums = (blocks, rows, width)
    if last:
        out_shape = [jax.ShapeDtypeStruct((rows + queries, width), CAST)] * blocks
        before = pltpu.with_memory_space_constraint(before, pltpu.HBM)
        inputs = [me, table] + list(early) + [late, before]
    else:
        out_shape = [jax.ShapeDtypeStruct((blocks, queries, width), CAST), pltpu.HBM(sums, jnp.float32)]
        inputs = [me, table] + list(early)
    extra_rows = min(entries, CAP * ((1 << levels) - 1)) * SUB
    list_rows = first_query + queries + levels * rows + extra_rows
    scratch = [
        pltpu.VMEM((blocks, rows, width), CAST),
        pltpu.VMEM((together, list_rows, queries), jnp.float32),
        pltpu.VMEM((together, extra_rows, width), CAST),
        pltpu.VMEM((together, list_rows, queries), CAST),
        pltpu.VMEM((together, list_rows, queries), CAST),
    ]
    scratch += [pltpu.VMEM(sums, jnp.float32)] * 2 + [pltpu.SemaphoreType.DMA((blocks,))]
    scratch.append(pltpu.VMEM((blocks, queries, width), CAST))
    pairs = blocks * (levels + 1) * rows * queries
    return pl.pallas_call(
        functools.partial(attention_kernel, blocks, rows, first_query, queries, together),
        out_shape=tuple(out_shape),
        in_specs=[small] * 2 + [whole] * (len(inputs) - 3) + [apart if last else whole],
        out_specs=(whole,) * (len(out_shape) - 1) + (whole if last else apart,),
        scratch_shapes=scratch,
        cost_estimate=pl.CostEstimate(flops=pairs * HD * 2 * 6 * 4, transcendentals=2 * pairs, bytes_accessed=8 << 20),
        compiler_params=pltpu.CompilerParams(vmem_limit_bytes=30 * 1024 * 1024),
    )(*inputs)


def swap(x):
    return jnp.concatenate([x[:, HD:], x[:, :HD]], axis=1)


def interleave(first, second):
    lane = lax.broadcasted_iota(jnp.int32, first.shape, 1)
    return jnp.where(lane < HD, first, swap(second)), jnp.where(lane < HD, swap(first), second)


def pack_kernel(heads, pieces, apart, count, *refs):
    me = refs[0][0]
    sources, results = refs[1 : 1 + count], refs[1 + count : -3]
    packed, inputs, arrived = refs[-3:]
    rows = sources[0].shape[0]
    parts = 2

    def copy(i, part):
        place = pl.ds(part * (rows // parts), rows // parts)
        return pltpu.make_async_copy(sources[i].at[place], inputs.at[i, place], arrived.at[i * parts + part])

    for i in range(count):
        for part in range(parts):
            copy(i, part).start()
    ready = set()
    at = 0
    for first, second, low, size in pieces:
        for i in (first, second):
            if i not in ready:
                for part in range(parts):
                    copy(i, part).wait()
                ready.add(i)
        for pair in range(heads // 2):
            lanes = slice(pair * 2 * HD, (pair + 1) * 2 * HD)
            both = interleave(inputs[first, low : low + size, lanes], inputs[second, low : low + size, lanes])
            packed[2 * pair, at : at + size, :] = both[0]
            packed[2 * pair + 1, at : at + size, :] = both[1]
        at += size
    if apart:
        for k, out in enumerate(results):
            out[...] = packed[wrapped(me + k, heads)]
    else:
        results[0][...] = packed[...]


def pack(me, arrays, pieces, apart):
    rows, columns = arrays[0].shape
    heads = columns // HD
    total = sum(piece[3] for piece in pieces)
    whole = pl.BlockSpec(memory_space=pltpu.VMEM)
    all_heads = (heads, total, 2 * HD)
    if apart:
        out_shape = (jax.ShapeDtypeStruct((total, 2 * HD), CAST),) * heads
        out_specs = (whole,) * heads
    else:
        out_shape, out_specs = jax.ShapeDtypeStruct(all_heads, CAST), whole
    return pl.pallas_call(
        functools.partial(pack_kernel, heads, pieces, apart, len(arrays)),
        out_shape=out_shape,
        in_specs=[pl.BlockSpec(memory_space=pltpu.SMEM)] + [pl.BlockSpec(memory_space=pltpu.HBM)] * len(arrays),
        out_specs=out_specs,
        scratch_shapes=[
            pltpu.VMEM(all_heads, CAST),
            pltpu.VMEM((len(arrays), rows, columns), CAST),
            pltpu.SemaphoreType.DMA((2 * len(arrays),)),
        ],
        compiler_params=pltpu.CompilerParams(vmem_limit_bytes=12 * 1024 * 1024),
        cost_estimate=pl.CostEstimate(flops=0, transcendentals=0, bytes_accessed=8 * total * heads * HD),
    )(me, *[pltpu.with_memory_space_constraint(array, pltpu.HBM) for array in arrays])


def unpack_kernel(heads, rows, *refs):
    me = refs[0][0]
    early, late = refs[1], refs[2 : 2 + heads]
    mixed, query_grad, key_grad, value_grad, ordered = refs[2 + heads :]
    for k in range(heads):
        ordered[wrapped(me - k, heads)] = late[k][...]
    half = early.shape[1]
    for pair in range(heads // 2):
        lanes = slice(pair * 2 * HD, (pair + 1) * 2 * HD)
        even, odd = ordered[2 * pair], ordered[2 * pair + 1]
        query_grad[:half, lanes], mixed[:half, lanes] = interleave(early[2 * pair], early[2 * pair + 1])
        query_grad[half:, lanes], mixed[half:, lanes] = interleave(even[rows:], odd[rows:])
        key_grad[:, lanes], value_grad[:, lanes] = interleave(even[:rows], odd[:rows])


def unpack(me, early, late, rows):
    heads = len(late)
    whole = pl.BlockSpec(memory_space=pltpu.VMEM)
    return pl.pallas_call(
        functools.partial(unpack_kernel, heads, rows),
        out_shape=(jax.ShapeDtypeStruct((rows, heads * HD), CAST),) * 4,
        in_specs=[pl.BlockSpec(memory_space=pltpu.SMEM)] + [whole] * (1 + heads),
        out_specs=(whole,) * 4,
        scratch_shapes=[pltpu.VMEM((heads,) + late[0].shape, CAST)],
        compiler_params=pltpu.CompilerParams(vmem_limit_bytes=10 * 1024 * 1024),
    )(me, early, *late)


def shifted_all(pieces):
    count = len(pieces)
    got = {0: pieces[0]}
    for k in sorted(range(1, count), key=lambda k: k):
        got[k] = lax.ppermute(pieces[k], "tm", [(i, (i + k) % count) for i in range(count)])
    return [got[k] for k in range(count)]


def all_heads(packed):
    return lax.all_to_all(packed, "tm", split_axis=0, concat_axis=0, tiled=True)


def head_plan(queries, key_rows, value_rows, grad_output, extra_blocks):
    rows = queries.shape[0]
    half = rows // 2
    me = lax.axis_index("tm").astype(jnp.int32).reshape(1)
    early = shifted_all(
        pack(me, (key_rows, value_rows, queries, grad_output), ((0, 1, 0, rows), (2, 3, 0, half)), True)
    )
    late_packed = pack(me, (queries, grad_output), ((0, 1, half, half),), False)
    *early[:4], late_packed = lax.optimization_barrier((*early[:4], late_packed))
    late = all_heads(late_packed)
    early_rows, sums = attention(me, extra_blocks, early, None, None, rows, 0, half)
    early_back = all_heads(early_rows)
    late_rows = attention(me, extra_blocks, early, late, sums, rows, half, half)
    late_back = shifted_all(late_rows)
    return unpack(me, early_back, late_back, rows)


def local(queries, key_rows, value_rows, grad_output, extra_blocks):
    if lax.axis_size("tm") == queries.shape[1] // HD:
        return head_plan(queries, key_rows, value_rows, grad_output, extra_blocks)
    return block_plan(queries, key_rows, value_rows, grad_output, extra_blocks)


def solution(mesh):
    placed = (
        P(("member", "tm"), None),
        P(("member", "tm"), None),
        P(("member", "tm"), None),
        P(("member", "tm"), None),
        P("member", None),
    )
    return jax.shard_map(
        local,
        mesh=mesh,
        in_specs=placed,
        out_specs=(
            P(("member", "tm"), None),
            P(("member", "tm"), None),
            P(("member", "tm"), None),
            P(("member", "tm"), None),
        ),
        check_vma=False,
    )
```
